128 devices in a mesh: virt: 16 (over y, z), occ: 8 (over x, core).
Axes of the slice: x: 4, y: 4, z: 4, core: 2. Of those that a mesh axis runs over, the one named last changes fastest.
Arguments:
- amplitudes: bfloat16 [64, 1024, 14400], P(None, ('virt', 'occ')), may hold values from -6 to 6
- integrals: bfloat16 [1024, 120, 960], P(('virt', 'occ')), may hold values from -0.046875 to 0.046875
- a_irrep: int32 [64], replicated, may hold values from 0 to 7
- b_irrep: int32 [8], replicated, may hold values from 0 to 7
- virt_irrep: int32 [1024], replicated, may hold values from 0 to 7, as said below
- occ_irrep: int32 [120], replicated, may hold values from 0 to 7, as said below
Outputs:
- cycle_term: float32 [64, 120, 960], P('virt', 'occ')
The draws below stay inside these ranges and needn't reach their ends.
Inputs may be any that keep to these rules, and one draw needn't show every extreme that they name: `virt_irrep`: nondecreasing along the 1024 virtuals (orbitals ordered by irrep, ragged blocks, some possibly empty); the first is 0 and the last 7. `occ_irrep`: nondecreasing along the 120 occupied orbitals (ragged blocks, some possibly empty); the first is 0 and the last 7.
All inputs are finite; a program needn't handle non-finite values.
Results may differ from the reference program's by a relative error of at most 0.0003.
Values may be sent and summed in bfloat16 or wider, within the bound.
No kernel may reach another device: no remote copies, remote signals or barrier semaphores. Data moves between devices by JAX's collectives and lax.ppermute only.
A program may use at most 192 MiB of HBM per device.

```python
import jax
import jax.numpy as jnp
from jax import lax

O = 120
V = 1024
BW = 8
AW = 64


def sorted_labels(key, length):
    cut_points = jnp.sort(jax.random.randint(key, (7,), 1, length))
    positions = jnp.arange(length, dtype=jnp.int32)
    return jnp.sum((positions[:, None] >= cut_points[None, :]).astype(jnp.int32), axis=1).astype(jnp.int32)


def draw_virt_irrep(key, part):
    key = jax.random.fold_in(key, 11)
    return sorted_labels(key, V)


def draw_occ_irrep(key, part):
    key = jax.random.fold_in(key, 12)
    return sorted_labels(key, O)


def plant(drawn, stream_key, low, largest):
    spot = [jax.random.randint(jax.random.fold_in(stream_key, axis), (), 0, length) for axis, length in enumerate(drawn.shape)]
    widest = drawn.shape.index(max(drawn.shape))
    neighbour = spot[:widest] + [(spot[widest] + 1) % drawn.shape[widest]] + spot[widest + 1:]
    return drawn.at[tuple(spot)].set(low).at[tuple(neighbour)].set(largest)


def level_of(own_key, extent, split, smallest, top_value):
    factor_of = 1.0
    for position, shards_of in split:
        draws = jax.random.uniform(jax.random.fold_in(jax.random.fold_in(own_key, 6), position), (shards_of,), jnp.float32, smallest / len(split), top_value / len(split))
        factor_of = factor_of * jnp.repeat(jnp.exp(draws), extent[position] // shards_of).reshape((-1,) + (1,) * (len(extent) - 1 - position))
    return factor_of


def bell_draw(key, dims, spread, bound, shards=(), kind=jnp.bfloat16):
    entries = spread * jax.random.normal(key, dims, jnp.float32)
    if shards:
        entries = entries * level_of(key, dims, shards, -0.22, 0.18)
    return jnp.clip(entries, -bound, bound).astype(kind)


def setup_inputs(seed: int = 0) -> dict:
    streams_of = jax.random.split(jax.random.key(seed), 7)
    return {
        "amplitudes": bell_draw(streams_of[0], (AW, V, O * O), 1.0, 6.0, ((1, 128),)),
        "integrals": bell_draw(streams_of[1], (V, O, BW * O), (V * O // 8) ** -0.5, 0.046875, ((0, 128),)),
        "a_irrep": plant(jax.random.randint(streams_of[2], (AW,), 0, 8), jax.random.fold_in(streams_of[2], 1), 0, 7).astype(jnp.int32),
        "b_irrep": plant(jax.random.randint(streams_of[3], (BW,), 0, 8), jax.random.fold_in(streams_of[3], 1), 0, 7).astype(jnp.int32),
        "virt_irrep": draw_virt_irrep(jax.random.fold_in(streams_of[6], 71), 0),
        "occ_irrep": draw_occ_irrep(jax.random.fold_in(streams_of[6], 71), 0),
    }


def pair_symmetry(left_labels, right_labels):
    return jnp.bitwise_xor(left_labels[:, None], right_labels[None, :])


def reference(amplitudes, integrals, a_irrep, b_irrep, virt_irrep, occ_irrep):
    slab_width = V // 16
    occ_pairs = pair_symmetry(occ_irrep, occ_irrep).reshape(-1)

    def accumulate(block_index, running):
        offset = (block_index * slab_width).astype(jnp.int32)
        amp_block = lax.dynamic_slice_in_dim(amplitudes, offset, slab_width, 1)
        label_block = lax.dynamic_slice_in_dim(virt_irrep, offset, slab_width, 0)
        keep_amp = pair_symmetry(a_irrep, label_block)[:, :, None] == occ_pairs[None, None, :]
        masked = jnp.where(keep_amp, amp_block, jnp.zeros((), amp_block.dtype))
        rows_first = masked.reshape(AW, slab_width, O, O).transpose(0, 2, 1, 3).reshape(AW * O, slab_width * O)
        int_block = lax.dynamic_slice_in_dim(integrals, offset, slab_width, 0).reshape(slab_width * O, BW * O)
        return running + jnp.dot(rows_first, int_block, preferred_element_type=jnp.float32)

    cycle_sum = lax.fori_loop(0, 16, accumulate, jnp.zeros((AW * O, BW * O), jnp.float32))
    row_sym = pair_symmetry(a_irrep, occ_irrep).reshape(-1)
    col_sym = pair_symmetry(b_irrep, occ_irrep).reshape(-1)
    keep_out = row_sym[:, None] == col_sym[None, :]
    cycle_term = jnp.where(keep_out, cycle_sum, jnp.zeros((), cycle_sum.dtype))
    return cycle_term.reshape(AW, O, BW * O)
```

```python
import jax
import jax.numpy as jnp
from jax import lax
from jax.experimental import pallas as pl
from jax.experimental.pallas import tpu as pltpu
from jax.sharding import Mesh, PartitionSpec as P

O = 120
BJ = 960
AW = 64
CAP = 255
LANES = 256
VMEM = 60 * 1024 * 1024


def quantized(rows):
    largest = jnp.max(jnp.abs(rows), axis=-1, keepdims=True)
    power = jnp.clip(jnp.floor(jnp.log2(largest * 1.001)) + 1.0, -100.0, 126.0)
    codes = jnp.round(rows * jnp.exp2(15.0 - power))
    lane = lax.broadcasted_iota(jnp.int32, rows.shape, rows.ndim - 1)
    return jnp.where(lane == LANES - 1, power, codes)

def contract_kernel(place, a_s, b_s, virt_s, occ_s, amp, ints, tail, occ_row, keep, send,
                    buf, wbuf, weights0, weights1, stage, labels, left0, left1, acc0, acc1, codes, sems, wsem, osem):
    device = place[0]; core = lax.rem(device, 2); first = place[1]
    wcopy = pltpu.make_async_copy(ints, wbuf, wsem)
    wcopy.start()
    def piece(q, g):
        start = 1920 * g + 512 * q
        size = 384 if q == 3 else 512
        if g == 7:
            if q >= 2: return None
            size = min(size, 14336 - start)
        return pltpu.make_async_copy(amp.at[:, :, pl.ds(start, size)], buf.at[:, :, pl.ds(start, size)], sems.at[q, g])
    copies = [[c for g in range(8) if (c := piece(q, g)) is not None] for q in range(4)]
    for q in range(4):
        for c in copies[q]: c.start()
    buf[:, :, 14336:] = tail[...]
    sub = lax.broadcasted_iota(jnp.int32, (8, 128), 0)
    e_label = jnp.zeros((8, 128), jnp.int32)
    e_scalars = [virt_s[device * 8 + e] for e in range(8)]
    for e in range(8):
        e_label = jnp.where(sub == e, e_scalars[e], e_label)
    def set_label(a, c):
        labels[a] = (e_label ^ a_s[a]).astype(labels.dtype)
        return c
    lax.fori_loop(0, AW, set_label, 0)
    turned = jnp.broadcast_to(occ_row[...], (128, 128))
    diag = lax.broadcasted_iota(jnp.int32, (128, 128), 0) == lax.broadcasted_iota(jnp.int32, (128, 128), 1)
    occ_col = jnp.sum(jnp.where(diag, turned, 0), axis=1, keepdims=True)[:O]
    x_lane = lax.broadcasted_iota(jnp.int32, (128, BJ), 1)
    m_sub = lax.broadcasted_iota(jnp.int32, (128, BJ), 0)
    x_row = lax.broadcasted_iota(jnp.int32, (1, BJ), 1)
    hit = jnp.zeros((128, BJ), jnp.bool_)
    occ_lane = jnp.zeros((1, BJ), jnp.int32)
    b_row = jnp.zeros((1, BJ), jnp.int32)
    for b in range(8):
        hit = hit | (x_lane - b * O == m_sub)
        b_row = jnp.where((x_row >= b * O), b_s[b], b_row)
    hit = hit & (m_sub < O)
    occ128 = jnp.sum(jnp.where(diag, turned, 0), axis=1, keepdims=True)
    class_row = jnp.sum(jnp.where(hit, occ128, 0), axis=0, keepdims=True) ^ b_row
    picks = []
    for part in range(8):
        shape = (O, BJ)
        mine = lax.broadcasted_iota(jnp.int32, shape, 0) + part * O
        other = lax.broadcasted_iota(jnp.int32, shape, 1)
        same = ((occ_col ^ b_s[part]) == class_row) & (other < mine)
        rank = jnp.sum(jnp.where(same, 1.0, 0.0), axis=1, keepdims=True) - first.astype(jnp.float32)
        slot = lax.broadcasted_iota(jnp.int32, (O, LANES), 1).astype(jnp.float32)
        chosen = (rank == slot) & (slot < CAP)
        picks.append(jnp.where(chosen, 1.0, 0.0))
    pick = jnp.concatenate(picks, axis=0).astype(jnp.bfloat16)
    wcopy.wait()
    for e in range(8):
        kept = jnp.where((occ_col ^ e_scalars[e]) == class_row, wbuf[e].astype(jnp.float32), 0.0)
        packed = jnp.dot(kept.astype(jnp.bfloat16), pick, preferred_element_type=jnp.float32)
        whole = jnp.concatenate([packed, jnp.zeros((128 - O, LANES), jnp.float32)], axis=0)
        weights0[e] = jnp.concatenate([whole, whole], axis=0).astype(jnp.bfloat16)
        weights1[e] = jnp.concatenate([whole[8:], whole, whole[:8]], axis=0).astype(jnp.bfloat16)

    lane = lax.broadcasted_iota(jnp.int32, (AW, 8, 128), 2)
    lane2 = lax.broadcasted_iota(jnp.int32, (8, 128), 1)
    occ8 = jnp.where(lane2 < O, jnp.broadcast_to(occ_row[...], (8, 128)), 64)

    def build(k, left):
        rolled = pltpu.roll(occ8, lax.rem(128 - 8 * k + 128, 128), axis=1)
        for g in range(8):
            tile = 15 * g + k
            now = buf[:, :, pl.ds(pl.multiple_of(jnp.minimum(tile, 112) * 128, 128), 128)]
            before = buf[:, :, pl.ds(pl.multiple_of(jnp.clip(tile - 1, 0, 112) * 128, 128), 128)]
            pair = (rolled ^ occ_s[jnp.minimum(16 * g + k, O - 1)])[None]
            merged = jnp.where(lane < O - 8 * k, now.astype(jnp.float32), before.astype(jnp.float32))
            merged = jnp.where(labels[...] == pair, merged, 0.0)
            for a in range(AW):
                stage[pl.ds(g * 520 + a, 8, stride=65), :] = merged[a]
            for e in range(8):
                rows = stage[pl.ds(g * 520 + 65 * e, 64), :]
                left[g * 64:(g + 1) * 64, e * 128:(e + 1) * 128] = rows.astype(jnp.bfloat16)

    def multiply(k, left, weights, acc):
        right = weights[:, pl.ds(pl.multiple_of(lax.div(k, 2) * 16, 16), 128), :]
        acc[...] = jnp.dot(left[...], right.reshape(1024, LANES), preferred_element_type=jnp.float32)

    def emit(k, acc):
        for g in range(8):
            i = 16 * g + k
            block = lax.div(i, 15)
            inner = i - block * 15
            ok = (k >= 0) & (i < O)
            x = jnp.where(ok, lax.div(block, 2), 4)
            inner = jnp.where(ok, inner, 0)
            slot = lax.rem(block + core, 2)
            codes[jnp.where(ok, slot, 0), x, inner] = quantized(acc[g * 64:(g + 1) * 64, :]).astype(jnp.int16)

    def wait(q):
        for c in copies[q]: c.wait()
    wait(0)
    acc1[...] = jnp.zeros_like(acc1)
    build(jnp.int32(0), left0)
    def turn(kk, carry):
        for q in range(1, 4):
            @pl.when(kk == 2 * q - 1)
            def _():
                wait(q)
        k = 2 * kk
        multiply(k, left0, weights0, acc0)
        build(k + 1, left1)
        emit(k - 1, acc1)
        multiply(k + 1, left1, weights1, acc1)
        build(jnp.minimum(k + 2, 15), left0)
        emit(k, acc0)
        return carry
    lax.fori_loop(0, 8, turn, 0)
    emit(jnp.int32(15), acc1)
    o1 = pltpu.make_async_copy(codes.at[0, pl.ds(0, 4)], keep, osem.at[0]); o1.start()
    o2 = pltpu.make_async_copy(codes.at[1, pl.ds(0, 4)], send, osem.at[1]); o2.start()
    o1.wait(); o2.wait()

def contract(place, a, b, virt, occ, amp, ints):
    any_ = pl.BlockSpec(memory_space=pl.ANY)
    vm = pl.BlockSpec(memory_space=pltpu.VMEM)
    sm = pl.BlockSpec(memory_space=pltpu.SMEM)
    occ_row = jnp.pad(occ, (0, 8))[None]
    return pl.pallas_call(
        contract_kernel,
        grid=(1,),
        in_specs=[sm] * 5 + [any_, any_, pl.BlockSpec((AW, 8, 128), lambda s: (0, 0, 112)), vm],
        out_specs=[any_, any_],
        scratch_shapes=[
            pltpu.VMEM((AW, 8, 113 * 128), jnp.bfloat16),
            pltpu.VMEM((8, O, BJ), jnp.bfloat16),
            pltpu.VMEM((8, 256, LANES), jnp.bfloat16),
            pltpu.VMEM((8, 256, LANES), jnp.bfloat16),
            pltpu.VMEM((4096+64, 128), jnp.float32),
            pltpu.VMEM((AW, 8, 128), jnp.int32),
            pltpu.VMEM((512, 1024), jnp.bfloat16),
            pltpu.VMEM((512, 1024), jnp.bfloat16),
            pltpu.VMEM((512, LANES), jnp.float32),
            pltpu.VMEM((512, LANES), jnp.float32),
            pltpu.VMEM((2, 5, 15, AW, LANES), jnp.int16),
            pltpu.SemaphoreType.DMA((4, 8)),
            pltpu.SemaphoreType.DMA,
            pltpu.SemaphoreType.DMA((2,)),
        ],
        out_shape=[
            jax.ShapeDtypeStruct((4, 15, AW, LANES), jnp.int16),
            jax.ShapeDtypeStruct((4, 15, AW, LANES), jnp.int16),
        ],
        compiler_params=pltpu.CompilerParams(vmem_limit_bytes=VMEM),
        name="contract",
    )(place, a, b, virt, occ, amp, ints, amp, occ_row)


def combined(one, two):
    one, two = one.astype(jnp.float32), two.astype(jnp.float32)
    power_one, power_two = one[..., LANES - 1 :], two[..., LANES - 1 :]
    power = jnp.maximum(power_one, power_two) + 1.0
    total = jnp.round(one * jnp.exp2(power_one - power) + two * jnp.exp2(power_two - power))
    lane = lax.broadcasted_iota(jnp.int32, one.shape, one.ndim - 1)
    return jnp.where(lane == LANES - 1, power, total)


def merge_kernel(own, came, out):
    for quad in range(4):
        sums = []
        for inner in range(4 * quad, min(4 * quad + 4, 15)):
            sums.append(combined(own[0, inner], came[0, inner]).reshape(8, 8, LANES))
        if quad == 3:
            sums.append(jnp.zeros_like(sums[0]))
        for half in range(2):
            rows = jnp.concatenate([s[:, 4 * half : 4 * half + 4] for s in sums], axis=1)
            out[:, half, 0, 16 * quad : 16 * quad + 16, :] = rows.astype(jnp.int16)


def merge(own, came):
    out = pl.pallas_call(
        merge_kernel,
        grid=(4,),
        in_specs=[pl.BlockSpec((1, 15, AW, LANES), lambda x: (x, 0, 0, 0))] * 2,
        out_specs=pl.BlockSpec((8, 2, 1, 64, LANES), lambda x: (0, 0, x, 0, 0)),
        out_shape=jax.ShapeDtypeStruct((8, 2, 4, 64, LANES), jnp.int16),
        compiler_params=pltpu.CompilerParams(vmem_limit_bytes=VMEM),
        name="merge",
    )(own, came)
    return out.reshape(64, 64, LANES)


def table_kernel(first, class_row, class_col, table):
    shape = (O, BJ)
    rank = jnp.zeros((1, BJ), jnp.float32)
    for part in range(8):
        before = lax.broadcasted_iota(jnp.int32, shape, 0) + part * O < lax.broadcasted_iota(jnp.int32, shape, 1)
        same = (class_col[part * O : (part + 1) * O, :] == class_row[...]) & before
        rank = rank + jnp.sum(jnp.where(same, 1.0, 0.0), axis=0, keepdims=True)
    slot = lax.broadcasted_iota(jnp.int32, (LANES, BJ), 0).astype(jnp.float32)
    chosen = (rank - first[0].astype(jnp.float32) == slot) & (slot < CAP)
    table[...] = jnp.where(chosen, 1.0, 0.0).astype(jnp.bfloat16)


def make_table(first, class_row, class_col):
    vm = pl.BlockSpec(memory_space=pltpu.VMEM)
    return pl.pallas_call(
        table_kernel,
        in_specs=[pl.BlockSpec(memory_space=pltpu.SMEM), vm, vm],
        out_specs=vm,
        out_shape=jax.ShapeDtypeStruct((LANES, BJ), jnp.bfloat16),
        compiler_params=pltpu.CompilerParams(vmem_limit_bytes=VMEM),
        name="table",
    )(first, class_row, class_col)


BATCH = 32


def expand_kernel(came, table, class_row, row_class, out, total):
    step = pl.program_id(0)
    part = jnp.zeros((64, LANES), jnp.float32)
    for n in range(BATCH):
        values = came[n].astype(jnp.float32)
        part = part + values * jnp.exp2(values[:, LANES - 1 :] - 15.0)

    @pl.when(step == 0)
    def _():
        total[...] = part

    @pl.when(step > 0)
    def _():
        total[...] = total[...] + part

    @pl.when(step == pl.num_programs(0) - 1)
    def _():
        lane = lax.broadcasted_iota(jnp.int32, (64, LANES), 1)
        value = jnp.where(lane == LANES - 1, 0.0, total[...])
        high = value.astype(jnp.bfloat16)
        rest = value - high.astype(jnp.float32)
        middle = rest.astype(jnp.bfloat16)
        low = (rest - middle.astype(jnp.float32)).astype(jnp.bfloat16)
        parts = jnp.concatenate([high, middle, low], axis=0)
        spread = jnp.dot(parts, table[...], preferred_element_type=jnp.float32)
        spread = spread[:64] + (spread[64:128] + spread[128:])
        out[...] = jnp.where(row_class[...] == class_row[...], spread, 0.0)[:60]


def expand(came, table, class_row, row_class):
    whole = lambda *shape: pl.BlockSpec(shape, lambda n: (0,) * len(shape))
    return pl.pallas_call(
        expand_kernel,
        grid=(64 // BATCH,),
        in_specs=[
            pl.BlockSpec((BATCH, 64, LANES), lambda n: (n, 0, 0)),
            whole(LANES, BJ),
            whole(1, BJ),
            whole(64, 1),
        ],
        out_specs=whole(60, BJ),
        out_shape=jax.ShapeDtypeStruct((60, BJ), jnp.float32),
        scratch_shapes=[pltpu.VMEM((64, LANES), jnp.float32)],
        compiler_params=pltpu.CompilerParams(vmem_limit_bytes=VMEM),
        name="expand",
    )(came, table, class_row, row_class)


def on_device(amplitudes, integrals, a_irrep, b_irrep, virt_irrep, occ_irrep):
    virt, x, core = lax.axis_index("virt"), lax.axis_index("x"), lax.axis_index("c")
    device = (virt * 4 + x) * 2 + core
    classes = (b_irrep[:, None] ^ occ_irrep[None, :]).reshape(BJ)
    class_row, class_col = classes[None, :], classes[:, None]
    a_rows = lax.dynamic_slice_in_dim(a_irrep, virt * 4, 4, 0)
    i_rows = lax.dynamic_slice_in_dim(occ_irrep, (2 * x + core) * 15, 15, 0)
    row_class = jnp.pad((i_rows[:, None] ^ a_rows[None, :]).reshape(60), (0, 4))[:, None]
    fullest = jnp.max(jnp.sum(classes[:, None] == jnp.arange(8)[None, :], axis=0))

    def one_pass(number):
        first = (number * CAP).astype(jnp.int32)
        place = jnp.stack([device, first]).astype(jnp.int32)
        keep, send = contract(place, a_irrep, b_irrep, virt_irrep, occ_irrep, amplitudes, integrals)
        came = lax.ppermute(send, "c", [(0, 1), (1, 0)])
        arrived = lax.all_to_all(merge(keep, came), ("virt", "x"), 0, 0, tiled=True)
        table = make_table(first[None], class_row, class_col)
        return expand(arrived, table, class_row, row_class)

    passes = lax.div(fullest + (CAP - 1), CAP)
    total = lax.fori_loop(1, passes, lambda n, total: total + one_pass(n), one_pass(jnp.int32(0)))
    return jnp.transpose(total.reshape(15, 4, BJ), (1, 0, 2))


def solution(mesh):
    fine = Mesh(mesh.devices.reshape(16, 4, 2), ("virt", "x", "c"))
    spread = ("virt", "x", "c")
    placed = (P(None, spread, None), P(spread, None, None), P(), P(), P(), P())
    return jax.shard_map(
        on_device, mesh=fine, in_specs=placed, out_specs=P("virt", ("x", "c"), None), check_vma=False
    )
```

```python
import functools

import jax
import jax.numpy as jnp
from jax import lax
from jax.experimental import pallas as pl
from jax.experimental.pallas import tpu as pltpu
from jax.sharding import Mesh, PartitionSpec as P

O = 120
BJ = 960
AW = 64
CAP = 256
LANES = 256
MIB = 1024 * 1024


GROUP = 5
ROWS = 15 * AW
CODED = ROWS + 16


def unit_codes(unit):
    unit = jnp.maximum(unit, 1e-30)
    power = jnp.floor(jnp.log2(unit)) - 13.0
    return power, jnp.floor(unit * jnp.exp2(-power)) + 1.0


def unit_of(power, mantissa):
    return mantissa * jnp.exp2(power)


def pack_rows(first, e_labels, b_s, ints, occ_line, weights):
    diagonal = lax.broadcasted_iota(jnp.int32, (128, 128), 0) == lax.broadcasted_iota(jnp.int32, (128, 128), 1)
    occ_col = jnp.sum(jnp.where(diagonal, jnp.broadcast_to(occ_line, (128, 128)), 0), axis=1, keepdims=True)
    lane = lax.broadcasted_iota(jnp.int32, (128, BJ), 1)
    row = lax.broadcasted_iota(jnp.int32, (128, BJ), 0)
    column = lax.broadcasted_iota(jnp.int32, (1, BJ), 1)
    hit = jnp.zeros((128, BJ), jnp.bool_)
    b_row = jnp.zeros((1, BJ), jnp.int32)
    for b in range(8):
        hit = hit | (lane - b * O == row)
        b_row = jnp.where(column >= b * O, b_s[b], b_row)
    hit = hit & (row < O)
    class_row = jnp.sum(jnp.where(hit, occ_col, 0), axis=0, keepdims=True) ^ b_row
    occ_col = occ_col[:O]
    picks = []
    for part in range(8):
        mine = lax.broadcasted_iota(jnp.int32, (O, BJ), 0) + part * O
        other = lax.broadcasted_iota(jnp.int32, (O, BJ), 1)
        same = ((occ_col ^ b_s[part]) == class_row) & (other < mine)
        rank = jnp.sum(jnp.where(same, 1.0, 0.0), axis=1, keepdims=True) - first.astype(jnp.float32)
        slot = lax.broadcasted_iota(jnp.int32, (O, LANES), 1).astype(jnp.float32)
        picks.append(jnp.where(rank == slot, 1.0, 0.0))
    pick = jnp.concatenate(picks, axis=0).astype(jnp.bfloat16)
    for e in range(8):
        kept = jnp.where((occ_col ^ e_labels[e]) == class_row, ints[e].astype(jnp.float32), 0.0)
        packed = jnp.dot(kept.astype(jnp.bfloat16), pick, preferred_element_type=jnp.float32)
        whole = jnp.concatenate([packed, jnp.zeros((128 - O, LANES), jnp.float32)], axis=0)
        weights[e * 128 : (e + 1) * 128, :] = whole.astype(jnp.bfloat16)


def contract_kernel(
    keeps, first, a_s, b_s, virt_s, occ_s, amp, edge, last, occ_in, source, *rest
):
    if keeps:
        out, buf, labels, stage, left, codes, lines, in_sems, out_sems = rest
        weights = source
    else:
        out, weights, buf, labels, stage, left, codes, lines, in_sems, out_sems, ints, ints_sem = rest
    core = lax.axis_index("c")
    device = (lax.axis_index("virt") * 4 + lax.axis_index("x")) * 2 + core
    half = core if keeps else 1 - core

    def read(x):
        start = pl.multiple_of(128 * (28 * x + 14 * half), 128)
        size = 1792 if x == 3 else 1920
        return pltpu.make_async_copy(
            amp.at[:, :, pl.ds(start, size)], buf.at[x, :, :, pl.ds(0, size)], in_sems.at[x]
        )

    reads = [read(x) for x in range(4)]
    e_labels = [virt_s[device * 8 + e] for e in range(8)]
    lines[...] = jnp.zeros_like(lines)
    lines[0:1, :O] = occ_in[...].astype(jnp.float32)
    occ_line = lines[0:1, :128].astype(jnp.int32)
    if not keeps:
        fetch = pltpu.make_async_copy(source, ints, ints_sem)
        fetch.start()
    reads[0].start()
    reads[1].start()
    row = lax.broadcasted_iota(jnp.int32, (8, 128), 0)
    e_label = jnp.zeros((8, 128), jnp.int32)
    for e in range(8):
        e_label = jnp.where(row == e, e_labels[e], e_label)
    for a in range(AW):
        labels[a] = e_label ^ a_s[a]
    buf[3, :, :, 1792:] = jnp.where(half == 0, edge[...], last[...])
    if not keeps:
        fetch.wait()
        pack_rows(first[0], e_labels, b_s, ints, occ_line, weights)
    lane = lax.broadcasted_iota(jnp.int32, (AW, 8, 128), 2)
    lanes = lax.broadcasted_iota(jnp.int32, (8, 128), 1)
    occ_rows = jnp.where(lanes < O, jnp.broadcast_to(occ_line, (8, 128)), 64)
    def write(x):
        return pltpu.make_async_copy(codes.at[x], out.at[x], out_sems.at[x])

    def block(x, carry):
        for n in range(4):

            @pl.when(x == n)
            def _():
                reads[n].wait()
                if n < 2:
                    reads[n + 2].start()

        for number in range(15 // GROUP):
            for u in range(GROUP):
                inner = number * GROUP + u
                flat = 16 * x + 8 * half + O * inner
                tile = lax.div(flat, 128)
                offset = flat - 128 * tile
                now = buf[x, :, :, pl.ds(pl.multiple_of(tile * 128, 128), 128)].astype(jnp.float32)
                after = buf[x, :, :, pl.ds(pl.multiple_of(tile * 128 + 128, 128), 128)].astype(jnp.float32)
                row = pltpu.roll(jnp.where(lane >= offset, now, after), lax.rem(128 - offset, 128), axis=2)
                pair = occ_rows ^ occ_s[30 * x + 15 * half + inner]
                row = jnp.where(labels[...] == pair[None], row, 0.0)
                for a in range(AW):
                    stage[number, pl.ds(u * 520 + a, 8, stride=65), :] = row[a]
                for e in range(8):
                    rows = stage[number, pl.ds(u * 520 + 65 * e, AW), :]
                    left[number, u * AW : (u + 1) * AW, e * 128 : (e + 1) * 128] = rows.astype(jnp.bfloat16)
            total = jnp.dot(left[number], weights[...], preferred_element_type=jnp.float32)
            largest = jnp.max(jnp.abs(total), axis=0, keepdims=True)
            power, mantissa = unit_codes(largest * (1.0001 / 32767.0))
            lines[2 * number : 2 * number + 1, :] = power
            lines[2 * number + 1 : 2 * number + 2, :] = mantissa
            coded = jnp.round(total * (1.0 / unit_of(power, mantissa)))
            codes[x, number * GROUP * AW : (number + 1) * GROUP * AW, :] = coded.astype(jnp.int16)
        codes[x, ROWS:, :] = jnp.concatenate([lines[...], lines[...]], axis=0).astype(jnp.int16)
        write(x).start()
        return carry

    lax.fori_loop(0, 4, block, 0)
    for x in range(4):
        write(x).wait()


def contract(keeps, first, a, b, virt, occ, amp, source):
    any_, sm, vm = (pl.BlockSpec(memory_space=space) for space in (pl.ANY, pltpu.SMEM, pltpu.VMEM))
    coded = jax.ShapeDtypeStruct((4, CODED, LANES), jnp.int16)
    packed = jax.ShapeDtypeStruct((1024, LANES), jnp.bfloat16)
    scratch = [
        pltpu.VMEM((4, AW, 8, 15 * 128), jnp.bfloat16),
        pltpu.VMEM((AW, 8, 128), jnp.int32),
        pltpu.VMEM((15 // GROUP, GROUP * 520, 128), jnp.float32),
        pltpu.VMEM((15 // GROUP, GROUP * AW, 1024), jnp.bfloat16),
        pltpu.VMEM((4, CODED, LANES), jnp.int16),
        pltpu.VMEM((8, LANES), jnp.float32),
        pltpu.SemaphoreType.DMA((4,)),
        pltpu.SemaphoreType.DMA((4,)),
    ]
    if not keeps:
        scratch += [pltpu.VMEM((8, O, BJ), jnp.bfloat16), pltpu.SemaphoreType.DMA]
    return pl.pallas_call(
        functools.partial(contract_kernel, keeps),
        grid=(1,),
        in_specs=[sm] * 5
        + [
            any_,
            pl.BlockSpec((AW, 8, 128), lambda s: (0, 0, 98)),
            pl.BlockSpec((AW, 8, 128), lambda s: (0, 0, 112)),
            vm,
            vm if keeps else any_,
        ],
        out_specs=any_ if keeps else [any_, vm],
        scratch_shapes=scratch,
        out_shape=coded if keeps else [coded, packed],
        cost_estimate=pl.CostEstimate(flops=8 * 10**9, bytes_accessed=12 * 10**6, transcendentals=0),
        compiler_params=pltpu.CompilerParams(vmem_limit_bytes=44 * MIB),
        name="contract_keep" if keeps else "contract_send",
    )(first, a, b, virt, occ, amp, amp, amp, occ[None], source)


def merge_kernel(own, came, out):
    own_lines = own[0, ROWS:, :].astype(jnp.float32)
    came_lines = came[0, ROWS:, :].astype(jnp.float32)
    units = []
    for g in range(3):
        units.append([unit_of(l[2 * g : 2 * g + 1], l[2 * g + 1 : 2 * g + 2]) for l in (own_lines, came_lines)])
    power, mantissa = unit_codes(1.0001 * jnp.maximum(jnp.maximum(sum(units[0]), sum(units[1])), sum(units[2])))
    inverse = 1.0 / unit_of(power, mantissa)
    codes = jnp.concatenate([power, mantissa, power, mantissa], axis=0)
    codes = jnp.broadcast_to(codes[None], (8, 4, LANES))
    for quad in range(4):
        sums = []
        for inner in range(4 * quad, min(4 * quad + 4, 15)):
            rows = slice(inner * AW, (inner + 1) * AW)
            one, two = (unit * inverse for unit in units[inner // GROUP])
            total = jnp.round(own[0, rows, :].astype(jnp.float32) * one + came[0, rows, :].astype(jnp.float32) * two)
            sums.append(total.reshape(8, 8, LANES))
        for half in range(2):
            rows = [s[:, 4 * half : 4 * half + 4] for s in sums] + ([codes] if quad == 3 else [])
            out[:, half, 0, 16 * quad : 16 * quad + 16, :] = jnp.concatenate(rows, axis=1).astype(jnp.int16)


def merge(own, came):
    out = pl.pallas_call(
        merge_kernel,
        grid=(4,),
        in_specs=[pl.BlockSpec((1, CODED, LANES), lambda x: (x, 0, 0))] * 2,
        out_specs=pl.BlockSpec((8, 2, 1, 64, LANES), lambda x: (0, 0, x, 0, 0)),
        out_shape=jax.ShapeDtypeStruct((8, 2, 4, 64, LANES), jnp.int16),
        compiler_params=pltpu.CompilerParams(vmem_limit_bytes=14 * MIB),
        name="merge",
    )(own, came)
    return out.reshape(64, 64, LANES)


def table_kernel(first, class_row, class_col, table):
    shape = (O, BJ)
    rank = jnp.zeros((1, BJ), jnp.float32)
    for part in range(8):
        before = lax.broadcasted_iota(jnp.int32, shape, 0) + part * O < lax.broadcasted_iota(jnp.int32, shape, 1)
        same = (class_col[part * O : (part + 1) * O, :] == class_row[...]) & before
        rank = rank + jnp.sum(jnp.where(same, 1.0, 0.0), axis=0, keepdims=True)
    slot = lax.broadcasted_iota(jnp.int32, (LANES, BJ), 0).astype(jnp.float32)
    chosen = rank - first[0].astype(jnp.float32) == slot
    table[...] = jnp.where(chosen, 1.0, 0.0).astype(jnp.bfloat16)


def make_table(first, class_row, class_col):
    vm = pl.BlockSpec(memory_space=pltpu.VMEM)
    return pl.pallas_call(
        table_kernel,
        in_specs=[pl.BlockSpec(memory_space=pltpu.SMEM), vm, vm],
        out_specs=vm,
        out_shape=jax.ShapeDtypeStruct((LANES, BJ), jnp.bfloat16),
        compiler_params=pltpu.CompilerParams(vmem_limit_bytes=14 * MIB),
        name="table",
    )(first, class_row, class_col)


BATCH = 32


def expand_kernel(came, table, class_row, row_class, out, total):
    step = pl.program_id(0)
    part = jnp.zeros((64, LANES), jnp.float32)
    for n in range(BATCH):
        values = came[n].astype(jnp.float32)
        part = part + values * unit_of(values[60:61], values[61:62])

    @pl.when(step == 0)
    def _():
        total[...] = part

    @pl.when(step > 0)
    def _():
        total[...] = total[...] + part

    @pl.when(step == pl.num_programs(0) - 1)
    def _():
        value = total[...]
        high = value.astype(jnp.bfloat16)
        rest = value - high.astype(jnp.float32)
        middle = rest.astype(jnp.bfloat16)
        low = (rest - middle.astype(jnp.float32)).astype(jnp.bfloat16)
        parts = jnp.concatenate([high, middle, low], axis=0)
        spread = jnp.dot(parts, table[...], preferred_element_type=jnp.float32)
        spread = spread[:64] + (spread[64:128] + spread[128:])
        out[...] = jnp.where(row_class[...] == class_row[...], spread, 0.0)[:60]


def expand(came, table, class_row, row_class):
    whole = lambda *shape: pl.BlockSpec(shape, lambda n: (0,) * len(shape))
    return pl.pallas_call(
        expand_kernel,
        grid=(64 // BATCH,),
        in_specs=[
            pl.BlockSpec((BATCH, 64, LANES), lambda n: (n, 0, 0)),
            whole(LANES, BJ),
            whole(1, BJ),
            whole(64, 1),
        ],
        out_specs=whole(60, BJ),
        out_shape=jax.ShapeDtypeStruct((60, BJ), jnp.float32),
        scratch_shapes=[pltpu.VMEM((64, LANES), jnp.float32)],
        compiler_params=pltpu.CompilerParams(vmem_limit_bytes=14 * MIB),
        name="expand",
    )(came, table, class_row, row_class)


def on_device(amplitudes, integrals, a_irrep, b_irrep, virt_irrep, occ_irrep):
    virt, x, core = lax.axis_index("virt"), lax.axis_index("x"), lax.axis_index("c")
    classes = (b_irrep[:, None] ^ occ_irrep[None, :]).reshape(BJ)
    class_row, class_col = classes[None, :], classes[:, None]
    a_rows = lax.dynamic_slice_in_dim(a_irrep, virt * 4, 4, 0)
    i_rows = lax.dynamic_slice_in_dim(occ_irrep, (2 * x + core) * 15, 15, 0)
    row_class = jnp.pad((i_rows[:, None] ^ a_rows[None, :]).reshape(60), (0, 4))[:, None]
    fullest = jnp.max(jnp.sum(classes[:, None] == jnp.arange(8)[None, :], axis=0))

    def one_pass(number):
        first = (number * CAP).astype(jnp.int32)[None]
        labels = a_irrep, b_irrep, virt_irrep, occ_irrep
        send, weights = contract(False, first, *labels, amplitudes, integrals)
        came = lax.ppermute(send, "c", [(0, 1), (1, 0)])
        keep = contract(True, first, *labels, amplitudes, weights)
        arrived = lax.all_to_all(merge(keep, came), ("virt", "x"), 0, 0, tiled=True)
        table = make_table(first, class_row, class_col)
        return expand(arrived, table, class_row, row_class)

    passes = lax.div(fullest + (CAP - 1), CAP)
    total = lax.fori_loop(1, passes, lambda n, total: total + one_pass(n), one_pass(jnp.int32(0)))
    return jnp.transpose(total.reshape(15, 4, BJ), (1, 0, 2))


def solution(mesh):
    fine = Mesh(mesh.devices.reshape(16, 4, 2), ("virt", "x", "c"))
    spread = ("virt", "x", "c")
    placed = (P(None, spread, None), P(spread, None, None), P(), P(), P(), P())
    return jax.shard_map(
        on_device, mesh=fine, in_specs=placed, out_specs=P("virt", ("x", "c"), None), check_vma=False
    )
```

```python
import functools

import jax
import jax.numpy as jnp
from jax import lax
from jax.experimental import pallas as pl
from jax.experimental.pallas import tpu as pltpu
from jax.sharding import Mesh, PartitionSpec as P

O = 120
BJ = 960
AW = 64
CAP = 256
LANES = 256
MIB = 1024 * 1024


GROUP = 5
ROWS = 15 * AW
CODED = ROWS + 16


def unit_codes(unit):
    unit = jnp.maximum(unit, 1e-30)
    power = jnp.floor(jnp.log2(unit)) - 13.0
    return power, jnp.floor(unit * jnp.exp2(-power)) + 1.0


def unit_of(power, mantissa):
    return mantissa * jnp.exp2(power)


def pack_rows(first, e_labels, b_s, ints, occ_line, weights, fullest):
    diagonal = lax.broadcasted_iota(jnp.int32, (128, 128), 0) == lax.broadcasted_iota(jnp.int32, (128, 128), 1)
    occ_col = jnp.sum(jnp.where(diagonal, jnp.broadcast_to(occ_line, (128, 128)), 0), axis=1, keepdims=True)
    lane = lax.broadcasted_iota(jnp.int32, (128, BJ), 1)
    row = lax.broadcasted_iota(jnp.int32, (128, BJ), 0)
    column = lax.broadcasted_iota(jnp.int32, (1, BJ), 1)
    hit = jnp.zeros((128, BJ), jnp.bool_)
    b_row = jnp.zeros((1, BJ), jnp.int32)
    for b in range(8):
        hit = hit | (lane - b * O == row)
        b_row = jnp.where(column >= b * O, b_s[b], b_row)
    hit = hit & (row < O)
    class_row = jnp.sum(jnp.where(hit, occ_col, 0), axis=0, keepdims=True) ^ b_row
    occ_col = occ_col[:O]
    picks = []
    highest = jnp.zeros((O, 1), jnp.float32)
    for part in range(8):
        mine = lax.broadcasted_iota(jnp.int32, (O, BJ), 0) + part * O
        other = lax.broadcasted_iota(jnp.int32, (O, BJ), 1)
        same = ((occ_col ^ b_s[part]) == class_row) & (other < mine)
        rank = jnp.sum(jnp.where(same, 1.0, 0.0), axis=1, keepdims=True)
        highest = jnp.maximum(highest, rank)
        slot = lax.broadcasted_iota(jnp.int32, (O, LANES), 1).astype(jnp.float32)
        picks.append(jnp.where(rank - first.astype(jnp.float32) == slot, 1.0, 0.0))
    fullest[0] = jnp.max(highest).astype(jnp.int32) + 1
    pick = jnp.concatenate(picks, axis=0).astype(jnp.bfloat16)
    for e in range(8):
        kept = jnp.where((occ_col ^ e_labels[e]) == class_row, ints[e].astype(jnp.float32), 0.0)
        packed = jnp.dot(kept.astype(jnp.bfloat16), pick, preferred_element_type=jnp.float32)
        whole = jnp.concatenate([packed, jnp.zeros((128 - O, LANES), jnp.float32)], axis=0)
        weights[e * 128 : (e + 1) * 128, :] = whole.astype(jnp.bfloat16)


def contract_kernel(
    keeps, first, a_s, b_s, virt_s, occ_s, amp, edge, last, occ_in, source, *rest
):
    if keeps:
        out, buf, labels, stage, left, codes, lines, in_sems, out_sems = rest
        weights = source
    else:
        out, weights, fullest, buf, labels, stage, left, codes, lines, in_sems, out_sems, ints, ints_sem = rest
    core = lax.axis_index("c")
    device = (lax.axis_index("virt") * 4 + lax.axis_index("x")) * 2 + core
    half = core if keeps else 1 - core

    def read(x):
        start = pl.multiple_of(128 * (28 * x + 14 * half), 128)
        size = 1792 if x == 3 else 1920
        return pltpu.make_async_copy(
            amp.at[:, :, pl.ds(start, size)], buf.at[x, :, :, pl.ds(0, size)], in_sems.at[x]
        )

    reads = [read(x) for x in range(4)]
    e_labels = [virt_s[device * 8 + e] for e in range(8)]
    lines[...] = jnp.zeros_like(lines)
    lines[0:1, :O] = occ_in[...].astype(jnp.float32)
    occ_line = lines[0:1, :128].astype(jnp.int32)
    if not keeps:
        fetch = pltpu.make_async_copy(source, ints, ints_sem)
        fetch.start()
    reads[0].start()
    reads[1].start()
    row = lax.broadcasted_iota(jnp.int32, (8, 128), 0)
    e_label = jnp.zeros((8, 128), jnp.int32)
    for e in range(8):
        e_label = jnp.where(row == e, e_labels[e], e_label)
    for a in range(AW):
        labels[a] = e_label ^ a_s[a]
    buf[3, :, :, 1792:] = jnp.where(half == 0, edge[...], last[...])
    if not keeps:
        fetch.wait()
        pack_rows(first[0], e_labels, b_s, ints, occ_line, weights, fullest)
    lane = lax.broadcasted_iota(jnp.int32, (AW, 8, 128), 2)
    lanes = lax.broadcasted_iota(jnp.int32, (8, 128), 1)
    occ_rows = jnp.where(lanes < O, jnp.broadcast_to(occ_line, (8, 128)), 64)
    def write(x):
        return pltpu.make_async_copy(codes.at[x], out.at[x], out_sems.at[x])

    def block(x, carry):
        for n in range(4):

            @pl.when(x == n)
            def _():
                reads[n].wait()
                if n < 2:
                    reads[n + 2].start()

        for number in range(15 // GROUP):
            for u in range(GROUP):
                inner = number * GROUP + u
                flat = 16 * x + 8 * half + O * inner
                tile = lax.div(flat, 128)
                offset = flat - 128 * tile
                now = buf[x, :, :, pl.ds(pl.multiple_of(tile * 128, 128), 128)].astype(jnp.float32)
                after = buf[x, :, :, pl.ds(pl.multiple_of(tile * 128 + 128, 128), 128)].astype(jnp.float32)
                row = pltpu.roll(jnp.where(lane >= offset, now, after), lax.rem(128 - offset, 128), axis=2)
                pair = occ_rows ^ occ_s[30 * x + 15 * half + inner]
                row = jnp.where(labels[...] == pair[None], row, 0.0)
                for a in range(AW):
                    stage[number, pl.ds(u * 520 + a, 8, stride=65), :] = row[a]
                for e in range(8):
                    rows = stage[number, pl.ds(u * 520 + 65 * e, AW), :]
                    left[number, u * AW : (u + 1) * AW, e * 128 : (e + 1) * 128] = rows.astype(jnp.bfloat16)
            total = jnp.dot(left[number], weights[...], preferred_element_type=jnp.float32)
            largest = jnp.max(jnp.abs(total), axis=0, keepdims=True)
            power, mantissa = unit_codes(largest * (1.0001 / 32767.0))
            lines[2 * number : 2 * number + 1, :] = power
            lines[2 * number + 1 : 2 * number + 2, :] = mantissa
            coded = jnp.round(total * (1.0 / unit_of(power, mantissa)))
            codes[x, number * GROUP * AW : (number + 1) * GROUP * AW, :] = coded.astype(jnp.int16)
        codes[x, ROWS:, :] = jnp.concatenate([lines[...], lines[...]], axis=0).astype(jnp.int16)
        write(x).start()
        return carry

    lax.fori_loop(0, 4, block, 0)
    for x in range(4):
        write(x).wait()


def contract(keeps, first, a, b, virt, occ, amp, source):
    any_, sm, vm = (pl.BlockSpec(memory_space=space) for space in (pl.ANY, pltpu.SMEM, pltpu.VMEM))
    coded = jax.ShapeDtypeStruct((4, CODED, LANES), jnp.int16)
    packed = jax.ShapeDtypeStruct((1024, LANES), jnp.bfloat16)
    scratch = [
        pltpu.VMEM((4, AW, 8, 15 * 128), jnp.bfloat16),
        pltpu.VMEM((AW, 8, 128), jnp.int32),
        pltpu.VMEM((15 // GROUP, GROUP * 520, 128), jnp.float32),
        pltpu.VMEM((15 // GROUP, GROUP * AW, 1024), jnp.bfloat16),
        pltpu.VMEM((4, CODED, LANES), jnp.int16),
        pltpu.VMEM((8, LANES), jnp.float32),
        pltpu.SemaphoreType.DMA((4,)),
        pltpu.SemaphoreType.DMA((4,)),
    ]
    if not keeps:
        scratch += [pltpu.VMEM((8, O, BJ), jnp.bfloat16), pltpu.SemaphoreType.DMA]
    return pl.pallas_call(
        functools.partial(contract_kernel, keeps),
        grid=(1,),
        in_specs=[sm] * 5
        + [
            any_,
            pl.BlockSpec((AW, 8, 128), lambda s: (0, 0, 98)),
            pl.BlockSpec((AW, 8, 128), lambda s: (0, 0, 112)),
            vm,
            vm if keeps else any_,
        ],
        out_specs=any_ if keeps else [any_, vm, sm],
        scratch_shapes=scratch,
        out_shape=coded if keeps else [coded, packed, jax.ShapeDtypeStruct((1,), jnp.int32)],
        cost_estimate=pl.CostEstimate(flops=8 * 10**9, bytes_accessed=12 * 10**6, transcendentals=0),
        compiler_params=pltpu.CompilerParams(vmem_limit_bytes=44 * MIB),
        name="contract_keep" if keeps else "contract_send",
    )(first, a, b, virt, occ, amp, amp, amp, occ[None], source)


def merge_kernel(own, came, out, more):
    own_lines = own[0, ROWS:, :].astype(jnp.float32)
    came_lines = came[0, ROWS:, :].astype(jnp.float32)
    units = []
    for g in range(3):
        units.append([unit_of(l[2 * g : 2 * g + 1], l[2 * g + 1 : 2 * g + 2]) for l in (own_lines, came_lines)])
    power, mantissa = unit_codes(1.0001 * jnp.maximum(jnp.maximum(sum(units[0]), sum(units[1])), sum(units[2])))
    inverse = 1.0 / unit_of(power, mantissa)
    codes = jnp.concatenate([power, mantissa, power, mantissa], axis=0)
    codes = jnp.broadcast_to(codes[None], (8, 4, LANES))
    wide_part = [[], []]
    for quad in range(4):
        sums = []
        for inner in range(4 * quad, min(4 * quad + 4, 15)):
            rows = slice(inner * AW, (inner + 1) * AW)
            one, two = (unit * inverse for unit in units[inner // GROUP])
            total = jnp.round(own[0, rows, :].astype(jnp.float32) * one + came[0, rows, :].astype(jnp.float32) * two)
            sums.append(total.reshape(8, 8, LANES))
        for half in range(2):
            rows = [s[:, 4 * half : 4 * half + 4] for s in sums] + ([codes] if quad == 3 else [])
            rows = jnp.concatenate(rows, axis=1)
            out[:, half, 0, 16 * quad : 16 * quad + 16, :] = rows[:, :, :128].astype(jnp.int16)
            wide_part[half].append(rows[:, :, 128:])
    lane = lax.broadcasted_iota(jnp.int32, (8, 16, 128), 2)
    for half in range(2):
        for quad in range(2):
            lower, upper = wide_part[half][quad], wide_part[half][quad + 2]
            turned = pltpu.roll(upper.reshape(128, 128), 64, axis=1).reshape(8, 16, 128)
            rows = jnp.where(lane < 64, lower, turned)
            out[:, half, 0, 64 + 16 * quad : 80 + 16 * quad, :] = rows.astype(jnp.int16)
            turned = pltpu.roll(lower.reshape(128, 128), 64, axis=1).reshape(8, 16, 128)
            rows = jnp.where(lane < 64, turned, upper)
            more[:, half, 0, 16 * quad : 16 * quad + 16, :] = rows.astype(jnp.int16)


def merge(own, came):
    shape = lambda rows: (8, 2, 4, rows, 128)
    out, more = pl.pallas_call(
        merge_kernel,
        grid=(4,),
        in_specs=[pl.BlockSpec((1, CODED, LANES), lambda x: (x, 0, 0))] * 2,
        out_specs=[pl.BlockSpec((8, 2, 1, rows, 128), lambda x: (0, 0, x, 0, 0)) for rows in (96, 32)],
        out_shape=[jax.ShapeDtypeStruct(shape(rows), jnp.int16) for rows in (96, 32)],
        compiler_params=pltpu.CompilerParams(vmem_limit_bytes=14 * MIB),
        name="merge",
    )(own, came)
    return out.reshape(64, 96, 128), more.reshape(64, 32, 128)


def table_kernel(first, class_row, class_col, table):
    shape = (O, BJ)
    rank = jnp.zeros((1, BJ), jnp.float32)
    for part in range(8):
        before = lax.broadcasted_iota(jnp.int32, shape, 0) + part * O < lax.broadcasted_iota(jnp.int32, shape, 1)
        same = (class_col[part * O : (part + 1) * O, :] == class_row[...]) & before
        rank = rank + jnp.sum(jnp.where(same, 1.0, 0.0), axis=0, keepdims=True)
    slot = lax.broadcasted_iota(jnp.int32, (LANES, BJ), 0).astype(jnp.float32)
    chosen = rank - first[0].astype(jnp.float32) == slot
    table[...] = jnp.where(chosen, 1.0, 0.0).astype(jnp.bfloat16)


def make_table(first, class_row, class_col):
    vm = pl.BlockSpec(memory_space=pltpu.VMEM)
    return pl.pallas_call(
        table_kernel,
        in_specs=[pl.BlockSpec(memory_space=pltpu.SMEM), vm, vm],
        out_specs=vm,
        out_shape=jax.ShapeDtypeStruct((LANES, BJ), jnp.bfloat16),
        compiler_params=pltpu.CompilerParams(vmem_limit_bytes=14 * MIB),
        name="table",
    )(first, class_row, class_col)


BATCH = 32


def expand_kernel(narrow, came, table, class_row, row_class, out, total):
    step = pl.program_id(0)
    part = jnp.zeros(came.shape[1:], jnp.float32)
    lane = lax.broadcasted_iota(jnp.int32, (1, 128), 1)
    for n in range(BATCH):
        values = came[n].astype(jnp.float32)
        parts = [values[:64] * unit_of(values[60:61], values[61:62])]
        unit = unit_of(values[92:93], values[93:94])
        turned = pltpu.roll(unit, 64, axis=1)
        parts.append(values[64:96] * jnp.where(lane < 64, turned, unit))
        if not narrow:
            unit = unit_of(values[124:125], values[125:126])
            turned = pltpu.roll(unit, 64, axis=1)
            parts.append(values[96:] * jnp.where(lane < 64, turned, unit))
        part = part + jnp.concatenate(parts, axis=0)

    @pl.when(step == 0)
    def _():
        total[...] = part

    @pl.when(step > 0)
    def _():
        total[...] = total[...] + part

    @pl.when(step == pl.num_programs(0) - 1)
    def _():
        value = total[...]
        third = jnp.concatenate([value[64:96], pltpu.roll(value[64:96], 64, axis=1)], axis=0)
        last = 0.0
        if not narrow:
            last = jnp.concatenate([pltpu.roll(value[96:], 64, axis=1), value[96:]], axis=0)
        value = jnp.concatenate([value[:64], jnp.where(lane < 64, third, last)], axis=1)
        high = value.astype(jnp.bfloat16)
        rest = value - high.astype(jnp.float32)
        middle = rest.astype(jnp.bfloat16)
        low = (rest - middle.astype(jnp.float32)).astype(jnp.bfloat16)
        parts = jnp.concatenate([high, middle, low], axis=0)
        spread = jnp.dot(parts, table[...], preferred_element_type=jnp.float32)
        spread = spread[:64] + (spread[64:128] + spread[128:])
        out[...] = jnp.where(row_class[...] == class_row[...], spread, 0.0)[:60]


def expand(narrow, came, table, class_row, row_class):
    whole = lambda *shape: pl.BlockSpec(shape, lambda n: (0,) * len(shape))
    sent = came.shape[1:]
    return pl.pallas_call(
        functools.partial(expand_kernel, narrow),
        grid=(64 // BATCH,),
        in_specs=[
            pl.BlockSpec((BATCH, *sent), lambda n: (n, 0, 0)),
            whole(LANES, BJ),
            whole(1, BJ),
            whole(64, 1),
        ],
        out_specs=whole(60, BJ),
        out_shape=jax.ShapeDtypeStruct((60, BJ), jnp.float32),
        scratch_shapes=[pltpu.VMEM(sent, jnp.float32)],
        compiler_params=pltpu.CompilerParams(vmem_limit_bytes=14 * MIB),
        name="expand_narrow" if narrow else "expand",
    )(came, table, class_row, row_class)


def on_device(amplitudes, integrals, a_irrep, b_irrep, virt_irrep, occ_irrep):
    virt, x, core = lax.axis_index("virt"), lax.axis_index("x"), lax.axis_index("c")
    labels = a_irrep, b_irrep, virt_irrep, occ_irrep

    def contracted(number):
        first = (number * CAP).astype(jnp.int32)[None]
        send, weights, fullest = contract(False, first, *labels, amplitudes, integrals)
        came = lax.ppermute(send, "c", [(0, 1), (1, 0)])
        return first, *merge(contract(True, first, *labels, amplitudes, weights), came), fullest[0]

    def finished(first, *coded):
        classes = (b_irrep[:, None] ^ occ_irrep[None, :]).reshape(BJ)
        class_row, class_col = classes[None, :], classes[:, None]
        a_rows = lax.dynamic_slice_in_dim(a_irrep, virt * 4, 4, 0)
        i_rows = lax.dynamic_slice_in_dim(occ_irrep, (2 * x + core) * 15, 15, 0)
        row_class = jnp.pad((i_rows[:, None] ^ a_rows[None, :]).reshape(60), (0, 4))[:, None]
        arrived = lax.all_to_all(jnp.concatenate(coded, axis=1), ("virt", "x"), 0, 0, tiled=True)
        return expand(len(coded) == 1, arrived, make_table(first, class_row, class_col), class_row, row_class)

    def all_passes(first, coded, more, fullest):
        def one_pass(number, total):
            first, coded, more, _ = contracted(number)
            return total + finished(first, coded, more)

        passes = lax.div(fullest + (CAP - 1), CAP)
        return lax.fori_loop(1, passes, one_pass, finished(first, coded, more))

    first, coded, more, fullest = contracted(jnp.int32(0))
    total = lax.cond(
        fullest <= 192,
        lambda first, coded, more, fullest: finished(first, coded),
        all_passes,
        first, coded, more, fullest,
    )
    return jnp.transpose(total.reshape(15, 4, BJ), (1, 0, 2))


def solution(mesh):
    fine = Mesh(mesh.devices.reshape(16, 4, 2), ("virt", "x", "c"))
    spread = ("virt", "x", "c")
    placed = (P(None, spread, None), P(spread, None, None), P(), P(), P(), P())
    return jax.shard_map(
        on_device, mesh=fine, in_specs=placed, out_specs=P("virt", ("x", "c"), None), check_vma=False
    )
```

```python
import functools

import jax
import jax.numpy as jnp
from jax import lax
from jax.experimental import pallas as pl
from jax.experimental.pallas import tpu as pltpu
from jax.sharding import Mesh, PartitionSpec as P

O = 120
BJ = 960
AW = 64
CAP = 256
LANES = 256
MIB = 1024 * 1024


GROUP = 5
ROWS = 15 * AW
CODED = ROWS + 16


def unit_codes(unit):
    unit = jnp.maximum(unit, 1e-30)
    power = jnp.floor(jnp.log2(unit)) - 13.0
    return power, jnp.floor(unit * jnp.exp2(-power)) + 1.0


def unit_of(power, mantissa):
    return mantissa * jnp.exp2(power)


def pack_rows(first, e_labels, b_s, ints, occ_line, weights, fullest):
    diagonal = lax.broadcasted_iota(jnp.int32, (128, 128), 0) == lax.broadcasted_iota(jnp.int32, (128, 128), 1)
    occ_col = jnp.sum(jnp.where(diagonal, jnp.broadcast_to(occ_line, (128, 128)), 0), axis=1, keepdims=True)
    lane = lax.broadcasted_iota(jnp.int32, (128, BJ), 1)
    row = lax.broadcasted_iota(jnp.int32, (128, BJ), 0)
    column = lax.broadcasted_iota(jnp.int32, (1, BJ), 1)
    hit = jnp.zeros((128, BJ), jnp.bool_)
    b_row = jnp.zeros((1, BJ), jnp.int32)
    for b in range(8):
        hit = hit | (lane - b * O == row)
        b_row = jnp.where(column >= b * O, b_s[b], b_row)
    hit = hit & (row < O)
    class_row = jnp.sum(jnp.where(hit, occ_col, 0), axis=0, keepdims=True) ^ b_row
    occ_col = occ_col[:O]
    picks = []
    highest = jnp.zeros((O, 1), jnp.float32)
    for part in range(8):
        mine = lax.broadcasted_iota(jnp.int32, (O, BJ), 0) + part * O
        other = lax.broadcasted_iota(jnp.int32, (O, BJ), 1)
        same = ((occ_col ^ b_s[part]) == class_row) & (other < mine)
        rank = jnp.sum(jnp.where(same, 1.0, 0.0), axis=1, keepdims=True)
        highest = jnp.maximum(highest, rank)
        slot = lax.broadcasted_iota(jnp.int32, (O, LANES), 1).astype(jnp.float32)
        picks.append(jnp.where(rank - first.astype(jnp.float32) == slot, 1.0, 0.0))
    fullest[0] = jnp.max(highest).astype(jnp.int32) + 1
    pick = jnp.concatenate(picks, axis=0).astype(jnp.bfloat16)
    for e in range(8):
        kept = jnp.where((occ_col ^ e_labels[e]) == class_row, ints[e].astype(jnp.float32), 0.0)
        packed = jnp.dot(kept.astype(jnp.bfloat16), pick, preferred_element_type=jnp.float32)
        whole = jnp.concatenate([packed, jnp.zeros((128 - O, LANES), jnp.float32)], axis=0)
        weights[e * 128 : (e + 1) * 128, :] = whole.astype(jnp.bfloat16)


def read_units(lines):
    return [unit_of(lines[2 * g : 2 * g + 1], lines[2 * g + 1 : 2 * g + 2]) for g in range(3)]


def contract_kernel(step, fused, first, a_s, b_s, virt_s, occ_s, amp, edge, last, occ_in, source, *rest):
    came = None
    if step is None:
        out, weights, fullest, buf, labels, stage, left, codes, lines, in_sems, out_sems, ints, ints_sem = rest
    elif fused:
        came, _, out, buf, labels, stage, left, codes, lines, in_sems, out_sems, other, other_sem = rest
        weights = source
    else:
        out, buf, labels, stage, left, codes, lines, in_sems, out_sems = rest
        weights = source
    core = lax.axis_index("c")
    my_x = lax.axis_index("x")
    device = (lax.axis_index("virt") * 4 + my_x) * 2 + core
    half = 1 - core if step is None else core
    target = None if step is None else lax.rem(my_x + step, 4)

    def read(x):
        start = pl.multiple_of(128 * (28 * x + 14 * half), 128)
        size = 1792 if x == 3 else 1920
        return pltpu.make_async_copy(
            amp.at[:, :, pl.ds(start, size)], buf.at[x, :, :, pl.ds(0, size)], in_sems.at[x]
        )

    if step is None:
        reads = [read(x) for x in range(4)]
    else:
        tile = 28 * target + 14 * half
        reads = [
            pltpu.make_async_copy(
                amp.at[:, :, pl.ds(pl.multiple_of(128 * tile, 128), 1792)],
                buf.at[0, :, :, pl.ds(0, 1792)],
                in_sems.at[0],
            ),
            pltpu.make_async_copy(
                amp.at[:, :, pl.ds(pl.multiple_of(128 * jnp.minimum(tile + 14, 111), 128), 128)],
                buf.at[0, :, :, pl.ds(1792, 128)],
                in_sems.at[1],
            ),
        ]
    e_labels = [virt_s[device * 8 + e] for e in range(8)]
    if step is None:
        fetch = pltpu.make_async_copy(source, ints, ints_sem)
        fetch.start()
    reads[0].start()
    reads[1].start()
    if fused:
        fetch = pltpu.make_async_copy(came.at[target], other, other_sem)
        fetch.start()
    lines[...] = jnp.zeros_like(lines)
    lines[0:1, :O] = occ_in[...].astype(jnp.float32)
    occ_line = lines[0:1, :128].astype(jnp.int32)
    row = lax.broadcasted_iota(jnp.int32, (8, 128), 0)
    e_label = jnp.zeros((8, 128), jnp.int32)
    for e in range(8):
        e_label = jnp.where(row == e, e_labels[e], e_label)
    for a in range(AW):
        labels[a] = e_label ^ a_s[a]
    if step is None:
        buf[3, :, :, 1792:] = jnp.where(half == 0, edge[...], last[...])
        fetch.wait()
        pack_rows(first[0], e_labels, b_s, ints, occ_line, weights, fullest)
    lane = lax.broadcasted_iota(jnp.int32, (AW, 8, 128), 2)
    lanes = lax.broadcasted_iota(jnp.int32, (8, 128), 1)
    occ_rows = jnp.where(lanes < O, jnp.broadcast_to(occ_line, (8, 128)), 64)

    def groups(x, slot, units):
        for number in range(15 // GROUP):
            for u in range(GROUP):
                inner = number * GROUP + u
                flat = 16 * x + 8 * half + O * inner
                tile = lax.div(flat, 128)
                offset = flat - 128 * tile
                now = buf[slot, :, :, pl.ds(pl.multiple_of(tile * 128, 128), 128)].astype(jnp.float32)
                after = buf[slot, :, :, pl.ds(pl.multiple_of(tile * 128 + 128, 128), 128)].astype(jnp.float32)
                row = pltpu.roll(jnp.where(lane >= offset, now, after), lax.rem(128 - offset, 128), axis=2)
                pair = occ_rows ^ occ_s[30 * x + 15 * half + inner]
                row = jnp.where(labels[...] == pair[None], row, 0.0)
                for a in range(AW):
                    stage[number, pl.ds(u * 520 + a, 8, stride=65), :] = row[a]
                for e in range(8):
                    rows = stage[number, pl.ds(u * 520 + 65 * e, AW), :]
                    left[number, u * AW : (u + 1) * AW, e * 128 : (e + 1) * 128] = rows.astype(jnp.bfloat16)
            mine = slice(number * GROUP * AW, (number + 1) * GROUP * AW)
            total = jnp.dot(left[number], weights[...], preferred_element_type=jnp.float32)
            if fused:
                total = total + other[mine, :].astype(jnp.float32) * units[number]
            largest = jnp.max(jnp.abs(total), axis=0, keepdims=True)
            power, mantissa = unit_codes(largest * (1.0001 / 32767.0))
            lines[2 * number : 2 * number + 1, :] = power
            lines[2 * number + 1 : 2 * number + 2, :] = mantissa
            coded = jnp.round(total * (1.0 / unit_of(power, mantissa)))
            codes[slot, mine, :] = coded.astype(jnp.int16)
        codes[slot, ROWS:, :] = jnp.concatenate([lines[...], lines[...]], axis=0).astype(jnp.int16)

    if step is not None:
        reads[0].wait()
        reads[1].wait()

        @pl.when((target == 3) & (half == 1))
        def _():
            buf[0, :, :, 1792:] = last[...]

        units = None
        if fused:
            fetch.wait()
            units = read_units(other[ROWS:, :].astype(jnp.float32))
        groups(target, 0, units)
        write = pltpu.make_async_copy(codes.at[0], out, out_sems.at[0])
        write.start()
        write.wait()
        return

    def write(x):
        return pltpu.make_async_copy(codes.at[x], out.at[x], out_sems.at[x])

    def block(x, carry):
        for n in range(4):

            @pl.when(x == n)
            def _():
                reads[n].wait()
                if n < 2:
                    reads[n + 2].start()

        groups(x, x, None)
        write(x).start()
        return carry

    lax.fori_loop(0, 4, block, 0)
    for x in range(4):
        write(x).wait()


def contract(step, first, a, b, virt, occ, amp, source, came=None, after=None):
    any_, sm, vm = (pl.BlockSpec(memory_space=space) for space in (pl.ANY, pltpu.SMEM, pltpu.VMEM))
    fused = came is not None
    blocks = 4 if step is None else 1
    coded = jax.ShapeDtypeStruct((4, CODED, LANES) if step is None else (CODED, LANES), jnp.int16)
    packed = jax.ShapeDtypeStruct((1024, LANES), jnp.bfloat16)
    scratch = [
        pltpu.VMEM((blocks, AW, 8, 15 * 128), jnp.bfloat16),
        pltpu.VMEM((AW, 8, 128), jnp.int32),
        pltpu.VMEM((15 // GROUP, GROUP * 520, 128), jnp.float32),
        pltpu.VMEM((15 // GROUP, GROUP * AW, 1024), jnp.bfloat16),
        pltpu.VMEM((blocks, CODED, LANES), jnp.int16),
        pltpu.VMEM((8, LANES), jnp.float32),
        pltpu.SemaphoreType.DMA((4,)),
        pltpu.SemaphoreType.DMA((4,)),
    ]
    if step is None:
        scratch += [pltpu.VMEM((8, O, BJ), jnp.bfloat16), pltpu.SemaphoreType.DMA]
    elif fused:
        scratch += [pltpu.VMEM((CODED, LANES), jnp.int16), pltpu.SemaphoreType.DMA]
    return pl.pallas_call(
        functools.partial(contract_kernel, step, fused),
        grid=(1,),
        in_specs=[sm] * 5
        + [
            any_,
            pl.BlockSpec((AW, 8, 128), lambda s: (0, 0, 98)),
            pl.BlockSpec((AW, 8, 128), lambda s: (0, 0, 112)),
            vm,
            any_ if step is None else vm,
        ]
        + ([any_, any_] if fused else []),
        out_specs=[any_, vm, sm] if step is None else any_,
        scratch_shapes=scratch,
        out_shape=[coded, packed, jax.ShapeDtypeStruct((1,), jnp.int32)] if step is None else coded,
        cost_estimate=pl.CostEstimate(flops=2 * 10**9 * blocks, bytes_accessed=3 * 10**6 * blocks, transcendentals=0),
        compiler_params=pltpu.CompilerParams(vmem_limit_bytes=(44 if step is None else 24) * MIB),
        name="contract_send" if step is None else "contract_keep_%d" % step,
    )(first, a, b, virt, occ, amp, amp, amp, occ[None], source, *((came, after) if fused else ()))


def pair_kernel(step, own, came, out, other, sem):
    target = lax.rem(lax.axis_index("x") + step, 4)
    fetch = pltpu.make_async_copy(came.at[target], other, sem)
    fetch.start()
    fetch.wait()
    units = [read_units(block[ROWS:, :].astype(jnp.float32)) for block in (own, other)]
    lines = []
    for g in range(3):
        power, mantissa = unit_codes(1.0001 * (units[0][g] + units[1][g]))
        inverse = 1.0 / unit_of(power, mantissa)
        lines += [power, mantissa]
        for n in range(GROUP):
            rows = slice((g * GROUP + n) * AW, (g * GROUP + n + 1) * AW)
            total = own[rows, :].astype(jnp.float32) * (units[0][g] * inverse)
            total = total + other[rows, :].astype(jnp.float32) * (units[1][g] * inverse)
            out[rows, :] = jnp.round(total).astype(jnp.int16)
    lines = jnp.concatenate(lines + lines + lines[:4], axis=0)
    out[ROWS:, :] = lines.astype(jnp.int16)


def pair(step, own, came):
    vm = pl.BlockSpec(memory_space=pltpu.VMEM)
    return pl.pallas_call(
        functools.partial(pair_kernel, step),
        in_specs=[vm, pl.BlockSpec(memory_space=pl.ANY)],
        out_specs=vm,
        out_shape=jax.ShapeDtypeStruct((CODED, LANES), jnp.int16),
        scratch_shapes=[pltpu.VMEM((CODED, LANES), jnp.int16), pltpu.SemaphoreType.DMA],
        compiler_params=pltpu.CompilerParams(vmem_limit_bytes=10 * MIB),
        name="pair",
    )(own, came)


def gather_kernel(one, two, three, four, out, more):
    blocks = (one, two, three, four)
    units = [read_units(block[ROWS:, :].astype(jnp.float32)) for block in blocks]
    bounds = [units[0][g] + units[1][g] + units[2][g] + units[3][g] for g in range(3)]
    power, mantissa = unit_codes(1.0001 * jnp.maximum(jnp.maximum(bounds[0], bounds[1]), bounds[2]))
    inverse = 1.0 / unit_of(power, mantissa)
    codes = jnp.concatenate([power, mantissa, power, mantissa], axis=0)
    codes = jnp.broadcast_to(codes[None], (8, 4, LANES))
    wide_part = [[], []]
    for quad in range(4):
        sums = []
        for inner in range(4 * quad, min(4 * quad + 4, 15)):
            rows = slice(inner * AW, (inner + 1) * AW)
            total = jnp.zeros((AW, LANES), jnp.float32)
            for block, unit in zip(blocks, units):
                total = total + block[rows, :].astype(jnp.float32) * (unit[inner // GROUP] * inverse)
            sums.append(jnp.round(total).reshape(8, 8, LANES))
        for half in range(2):
            rows = [s[:, 4 * half : 4 * half + 4] for s in sums] + ([codes] if quad == 3 else [])
            rows = jnp.concatenate(rows, axis=1)
            out[:, half, 16 * quad : 16 * quad + 16, :] = rows[:, :, :128].astype(jnp.int16)
            wide_part[half].append(rows[:, :, 128:])
    lane = lax.broadcasted_iota(jnp.int32, (8, 16, 128), 2)
    for half in range(2):
        for quad in range(2):
            lower, upper = wide_part[half][quad], wide_part[half][quad + 2]
            turned = pltpu.roll(upper.reshape(128, 128), 64, axis=1).reshape(8, 16, 128)
            rows = jnp.where(lane < 64, lower, turned)
            out[:, half, 64 + 16 * quad : 80 + 16 * quad, :] = rows.astype(jnp.int16)
            turned = pltpu.roll(lower.reshape(128, 128), 64, axis=1).reshape(8, 16, 128)
            rows = jnp.where(lane < 64, turned, upper)
            more[:, half, 16 * quad : 16 * quad + 16, :] = rows.astype(jnp.int16)


def gather(*blocks):
    vm = pl.BlockSpec(memory_space=pltpu.VMEM)
    out, more = pl.pallas_call(
        gather_kernel,
        in_specs=[vm] * 4,
        out_specs=[vm, vm],
        out_shape=[jax.ShapeDtypeStruct((8, 2, rows, 128), jnp.int16) for rows in (96, 32)],
        compiler_params=pltpu.CompilerParams(vmem_limit_bytes=14 * MIB),
        name="gather",
    )(*blocks)
    return out.reshape(16, 96, 128), more.reshape(16, 32, 128)


def table_kernel(first, class_row, class_col, table):
    shape = (O, BJ)
    rank = jnp.zeros((1, BJ), jnp.float32)
    for part in range(8):
        before = lax.broadcasted_iota(jnp.int32, shape, 0) + part * O < lax.broadcasted_iota(jnp.int32, shape, 1)
        same = (class_col[part * O : (part + 1) * O, :] == class_row[...]) & before
        rank = rank + jnp.sum(jnp.where(same, 1.0, 0.0), axis=0, keepdims=True)
    slot = lax.broadcasted_iota(jnp.int32, (LANES, BJ), 0).astype(jnp.float32)
    chosen = rank - first[0].astype(jnp.float32) == slot
    table[...] = jnp.where(chosen, 1.0, 0.0).astype(jnp.bfloat16)


def make_table(first, class_row, class_col):
    vm = pl.BlockSpec(memory_space=pltpu.VMEM)
    return pl.pallas_call(
        table_kernel,
        in_specs=[pl.BlockSpec(memory_space=pltpu.SMEM), vm, vm],
        out_specs=vm,
        out_shape=jax.ShapeDtypeStruct((LANES, BJ), jnp.bfloat16),
        compiler_params=pltpu.CompilerParams(vmem_limit_bytes=14 * MIB),
        name="table",
    )(first, class_row, class_col)


BATCH = 8


def expand_kernel(narrow, came, table, class_row, row_class, out, total):
    step = pl.program_id(0)
    part = jnp.zeros(came.shape[1:], jnp.float32)
    lane = lax.broadcasted_iota(jnp.int32, (1, 128), 1)
    for n in range(BATCH):
        values = came[n].astype(jnp.float32)
        parts = [values[:64] * unit_of(values[60:61], values[61:62])]
        unit = unit_of(values[92:93], values[93:94])
        turned = pltpu.roll(unit, 64, axis=1)
        parts.append(values[64:96] * jnp.where(lane < 64, turned, unit))
        if not narrow:
            unit = unit_of(values[124:125], values[125:126])
            turned = pltpu.roll(unit, 64, axis=1)
            parts.append(values[96:] * jnp.where(lane < 64, turned, unit))
        part = part + jnp.concatenate(parts, axis=0)

    @pl.when(step == 0)
    def _():
        total[...] = part

    @pl.when(step > 0)
    def _():
        total[...] = total[...] + part

    @pl.when(step == pl.num_programs(0) - 1)
    def _():
        value = total[...]
        third = jnp.concatenate([value[64:96], pltpu.roll(value[64:96], 64, axis=1)], axis=0)
        last = 0.0
        if not narrow:
            last = jnp.concatenate([pltpu.roll(value[96:], 64, axis=1), value[96:]], axis=0)
        value = jnp.concatenate([value[:64], jnp.where(lane < 64, third, last)], axis=1)
        high = value.astype(jnp.bfloat16)
        rest = value - high.astype(jnp.float32)
        middle = rest.astype(jnp.bfloat16)
        low = (rest - middle.astype(jnp.float32)).astype(jnp.bfloat16)
        parts = jnp.concatenate([high, middle, low], axis=0)
        spread = jnp.dot(parts, table[...], preferred_element_type=jnp.float32)
        spread = spread[:64] + (spread[64:128] + spread[128:])
        out[...] = jnp.where(row_class[...] == class_row[...], spread, 0.0)[:60].reshape(15, 4, BJ)


def expand(narrow, came, table, class_row, row_class):
    whole = lambda *shape: pl.BlockSpec(shape, lambda n: (0,) * len(shape))
    sent = came.shape[1:]
    return pl.pallas_call(
        functools.partial(expand_kernel, narrow),
        grid=(came.shape[0] // BATCH,),
        in_specs=[
            pl.BlockSpec((BATCH, *sent), lambda n: (n, 0, 0)),
            whole(LANES, BJ),
            whole(1, BJ),
            whole(64, 1),
        ],
        out_specs=whole(15, 4, BJ),
        out_shape=jax.ShapeDtypeStruct((15, 4, BJ), jnp.float32),
        scratch_shapes=[pltpu.VMEM(sent, jnp.float32)],
        compiler_params=pltpu.CompilerParams(vmem_limit_bytes=14 * MIB),
        name="expand_narrow" if narrow else "expand",
    )(came, table, class_row, row_class)


def on_device(amplitudes, integrals, a_irrep, b_irrep, virt_irrep, occ_irrep):
    virt, x, core = lax.axis_index("virt"), lax.axis_index("x"), lax.axis_index("c")
    labels = a_irrep, b_irrep, virt_irrep, occ_irrep

    def contracted(number):
        first = (number * CAP).astype(jnp.int32)[None]
        send, weights, fullest = contract(None, first, *labels, amplitudes, integrals)
        came = lax.ppermute(send, "c", [(0, 1), (1, 0)])
        ahead = lambda step, block: lax.ppermute(block, "x", [(n, (n + step) % 4) for n in range(4)])
        two = pair(2, contract(2, first, *labels, amplitudes, weights), came)
        one = contract(1, first, *labels, amplitudes, weights, came, two)
        three = contract(3, first, *labels, amplitudes, weights, came, one)
        own = contract(0, first, *labels, amplitudes, weights, came, three)
        return first, *gather(own, ahead(2, two), ahead(1, one), ahead(3, three)), fullest[0]

    def finished(first, *coded):
        classes = (b_irrep[:, None] ^ occ_irrep[None, :]).reshape(BJ)
        class_row, class_col = classes[None, :], classes[:, None]
        a_rows = lax.dynamic_slice_in_dim(a_irrep, virt * 4, 4, 0)
        i_rows = lax.dynamic_slice_in_dim(occ_irrep, (2 * x + core) * 15, 15, 0)
        row_class = jnp.pad((i_rows[:, None] ^ a_rows[None, :]).reshape(60), (0, 4))[:, None]
        arrived = lax.all_to_all(jnp.concatenate(coded, axis=1), "virt", 0, 0, tiled=True)
        return expand(len(coded) == 1, arrived, make_table(first, class_row, class_col), class_row, row_class)

    def all_passes(first, coded, more, fullest):
        def one_pass(number, total):
            first, coded, more, _ = contracted(number)
            return total + finished(first, coded, more)

        passes = lax.div(fullest + (CAP - 1), CAP)
        return lax.fori_loop(1, passes, one_pass, finished(first, coded, more))

    first, coded, more, fullest = contracted(jnp.int32(0))
    total = lax.cond(
        fullest <= 192,
        lambda first, coded, more, fullest: finished(first, coded),
        all_passes,
        first, coded, more, fullest,
    )
    return jnp.transpose(total, (1, 0, 2))


def solution(mesh):
    fine = Mesh(mesh.devices.reshape(16, 4, 2), ("virt", "x", "c"))
    spread = ("virt", "x", "c")
    placed = (P(None, spread, None), P(spread, None, None), P(), P(), P(), P())
    return jax.shard_map(
        on_device, mesh=fine, in_specs=placed, out_specs=P("virt", ("x", "c"), None), check_vma=False
    )
```

```python
import functools

import jax
import jax.numpy as jnp
from jax import lax
from jax.experimental import pallas as pl
from jax.experimental.pallas import tpu as pltpu
from jax.sharding import Mesh, PartitionSpec as P

O = 120
BJ = 960
AW = 64
CAP = 256
LANES = 256
MIB = 1024 * 1024


GROUP = 5
ROWS = 15 * AW
CODED = ROWS + 16


def unit_codes(unit):
    unit = jnp.maximum(unit, 1e-30)
    power = jnp.floor(jnp.log2(unit)) - 13.0
    return power, jnp.floor(unit * jnp.exp2(-power)) + 1.0


def unit_of(power, mantissa):
    return mantissa * jnp.exp2(power)


def pack_rows(first, e_labels, b_s, ints, occ_line, weights, fullest):
    diagonal = lax.broadcasted_iota(jnp.int32, (128, 128), 0) == lax.broadcasted_iota(jnp.int32, (128, 128), 1)
    occ_col = jnp.sum(jnp.where(diagonal, jnp.broadcast_to(occ_line, (128, 128)), 0), axis=1, keepdims=True)
    lane = lax.broadcasted_iota(jnp.int32, (128, BJ), 1)
    row = lax.broadcasted_iota(jnp.int32, (128, BJ), 0)
    column = lax.broadcasted_iota(jnp.int32, (1, BJ), 1)
    hit = jnp.zeros((128, BJ), jnp.bool_)
    b_row = jnp.zeros((1, BJ), jnp.int32)
    for b in range(8):
        hit = hit | (lane - b * O == row)
        b_row = jnp.where(column >= b * O, b_s[b], b_row)
    hit = hit & (row < O)
    class_row = jnp.sum(jnp.where(hit, occ_col, 0), axis=0, keepdims=True) ^ b_row
    occ_col = occ_col[:O]
    picks = []
    highest = jnp.zeros((O, 1), jnp.float32)
    for part in range(8):
        mine = lax.broadcasted_iota(jnp.int32, (O, BJ), 0) + part * O
        other = lax.broadcasted_iota(jnp.int32, (O, BJ), 1)
        same = ((occ_col ^ b_s[part]) == class_row) & (other < mine)
        rank = jnp.sum(jnp.where(same, 1.0, 0.0), axis=1, keepdims=True)
        highest = jnp.maximum(highest, rank)
        slot = lax.broadcasted_iota(jnp.int32, (O, LANES), 1).astype(jnp.float32)
        picks.append(jnp.where(rank - first.astype(jnp.float32) == slot, 1.0, 0.0))
    fullest[0] = jnp.max(highest).astype(jnp.int32) + 1
    pick = jnp.concatenate(picks, axis=0).astype(jnp.bfloat16)
    for e in range(8):
        kept = jnp.where((occ_col ^ e_labels[e]) == class_row, ints[e].astype(jnp.float32), 0.0)
        packed = jnp.dot(kept.astype(jnp.bfloat16), pick, preferred_element_type=jnp.float32)
        whole = jnp.concatenate([packed, jnp.zeros((128 - O, LANES), jnp.float32)], axis=0)
        weights[e * 128 : (e + 1) * 128, :] = whole.astype(jnp.bfloat16)


NARROW = CODED + ROWS // 2 + 16


def doubled(rows):
    lane = lax.broadcasted_iota(jnp.int32, rows.shape, 1)
    return jnp.where(lane < 64, rows, pltpu.roll(rows, 64, axis=1))


def read_units(block):
    narrow = block.shape[0] == NARROW
    lines = block[ROWS:CODED, :].astype(jnp.float32)
    if narrow:
        lines = jnp.concatenate([lines, block[NARROW - 16 :, :].astype(jnp.float32)], axis=1)
    return [unit_of(lines[2 * g : 2 * g + 1], lines[2 * g + 1 : 2 * g + 2]) for g in range(3)]


def put_rows(out, group, coded):
    size = GROUP * AW
    if out.shape[0] == CODED:
        out[group * size : (group + 1) * size, :] = coded.astype(jnp.int16)
        return
    out[group * size : (group + 1) * size, :] = coded[:, :128].astype(jnp.int16)
    high = coded[:, 128:].reshape(GROUP, AW, 128)
    lower, upper = (part.reshape(size // 2, 128) for part in (high[:, :32], high[:, 32:]))
    lane = lax.broadcasted_iota(jnp.int32, lower.shape, 1)
    rows = jnp.where(lane < 64, lower, pltpu.roll(upper, 64, axis=1))
    start = CODED + group * size // 2
    out[start : start + size // 2, :] = rows.astype(jnp.int16)


def put_units(out, lines):
    lines = jnp.concatenate([lines, lines], axis=0)
    if out.shape[0] == CODED:
        out[ROWS:, :] = lines.astype(jnp.int16)
        return
    out[ROWS:CODED, :] = lines[:, :128].astype(jnp.int16)
    out[NARROW - 16 :, :] = doubled(lines[:, 128:]).astype(jnp.int16)


def contract_kernel(step, fused, first, a_s, b_s, virt_s, occ_s, amp, edge, last, occ_in, source, *rest):
    came = None
    if step is None:
        out, weights, fullest, buf, labels, stage, left, codes, lines, in_sems, out_sems, ints, ints_sem = rest
    elif fused:
        came, _, out, buf, labels, stage, left, codes, lines, in_sems, out_sems, other, other_sem = rest
        weights = source
    else:
        out, buf, labels, stage, left, codes, lines, in_sems, out_sems = rest
        weights = source
    core = lax.axis_index("c")
    my_x = lax.axis_index("x")
    device = (lax.axis_index("virt") * 4 + my_x) * 2 + core
    half = 1 - core if step is None else core
    target = None if step is None else lax.rem(my_x + step, 4)

    def read(x):
        start = pl.multiple_of(128 * (28 * x + 14 * half), 128)
        size = 1792 if x == 3 else 1920
        return pltpu.make_async_copy(
            amp.at[:, :, pl.ds(start, size)], buf.at[x, :, :, pl.ds(0, size)], in_sems.at[x]
        )

    if step is None:
        reads = [read(x) for x in range(4)]
    else:
        tile = 28 * target + 14 * half
        reads = [
            pltpu.make_async_copy(
                amp.at[:, :, pl.ds(pl.multiple_of(128 * tile, 128), 1792)],
                buf.at[0, :, :, pl.ds(0, 1792)],
                in_sems.at[0],
            ),
            pltpu.make_async_copy(
                amp.at[:, :, pl.ds(pl.multiple_of(128 * jnp.minimum(tile + 14, 111), 128), 128)],
                buf.at[0, :, :, pl.ds(1792, 128)],
                in_sems.at[1],
            ),
        ]
    e_labels = [virt_s[device * 8 + e] for e in range(8)]
    if step is None:
        fetch = pltpu.make_async_copy(source, ints, ints_sem)
        fetch.start()
    reads[0].start()
    reads[1].start()
    if fused:
        fetch = pltpu.make_async_copy(came.at[target], other, other_sem)
        fetch.start()
    lines[...] = jnp.zeros_like(lines)
    lines[0:1, :O] = occ_in[...].astype(jnp.float32)
    occ_line = lines[0:1, :128].astype(jnp.int32)
    row = lax.broadcasted_iota(jnp.int32, (8, 128), 0)
    e_label = jnp.zeros((8, 128), jnp.int32)
    for e in range(8):
        e_label = jnp.where(row == e, e_labels[e], e_label)
    for a in range(AW):
        labels[a] = e_label ^ a_s[a]
    if step is None:
        buf[3, :, :, 1792:] = jnp.where(half == 0, edge[...], last[...])
        fetch.wait()
        pack_rows(first[0], e_labels, b_s, ints, occ_line, weights, fullest)
    lane = lax.broadcasted_iota(jnp.int32, (AW, 8, 128), 2)
    lanes = lax.broadcasted_iota(jnp.int32, (8, 128), 1)
    occ_rows = jnp.where(lanes < O, jnp.broadcast_to(occ_line, (8, 128)), 64)

    def groups(x, slot, units):
        for number in range(15 // GROUP):
            for u in range(GROUP):
                inner = number * GROUP + u
                flat = 16 * x + 8 * half + O * inner
                tile = lax.div(flat, 128)
                offset = flat - 128 * tile
                now = buf[slot, :, :, pl.ds(pl.multiple_of(tile * 128, 128), 128)].astype(jnp.float32)
                after = buf[slot, :, :, pl.ds(pl.multiple_of(tile * 128 + 128, 128), 128)].astype(jnp.float32)
                row = pltpu.roll(jnp.where(lane >= offset, now, after), lax.rem(128 - offset, 128), axis=2)
                pair = occ_rows ^ occ_s[30 * x + 15 * half + inner]
                row = jnp.where(labels[...] == pair[None], row, 0.0)
                for a in range(AW):
                    stage[number, pl.ds(u * 520 + a, 8, stride=65), :] = row[a]
                for e in range(8):
                    rows = stage[number, pl.ds(u * 520 + 65 * e, AW), :]
                    left[number, u * AW : (u + 1) * AW, e * 128 : (e + 1) * 128] = rows.astype(jnp.bfloat16)
            mine = slice(number * GROUP * AW, (number + 1) * GROUP * AW)
            total = jnp.dot(left[number], weights[...], preferred_element_type=jnp.float32)
            if fused:
                total = total + other[mine, :].astype(jnp.float32) * units[number]
            largest = jnp.max(jnp.abs(total), axis=0, keepdims=True)
            power, mantissa = unit_codes(largest * (1.0001 / 32767.0))
            lines[2 * number : 2 * number + 1, :] = power
            lines[2 * number + 1 : 2 * number + 2, :] = mantissa
            coded = jnp.round(total * (1.0 / unit_of(power, mantissa)))
            put_rows(codes.at[slot], number, coded)
        put_units(codes.at[slot], lines[...])

    if step is not None:
        reads[0].wait()
        reads[1].wait()

        @pl.when((target == 3) & (half == 1))
        def _():
            buf[0, :, :, 1792:] = last[...]

        units = None
        if fused:
            fetch.wait()
            units = read_units(other)
        groups(target, 0, units)
        write = pltpu.make_async_copy(codes.at[0], out, out_sems.at[0])
        write.start()
        write.wait()
        return

    def write(x):
        return pltpu.make_async_copy(codes.at[x], out.at[x], out_sems.at[x])

    def block(x, carry):
        for n in range(4):

            @pl.when(x == n)
            def _():
                reads[n].wait()
                if n < 2:
                    reads[n + 2].start()

        groups(x, x, None)
        write(x).start()
        return carry

    lax.fori_loop(0, 4, block, 0)
    for x in range(4):
        write(x).wait()


def contract(step, first, a, b, virt, occ, amp, source, came=None, after=None, narrow=False):
    any_, sm, vm = (pl.BlockSpec(memory_space=space) for space in (pl.ANY, pltpu.SMEM, pltpu.VMEM))
    fused = came is not None
    blocks = 4 if step is None else 1
    shape = (NARROW, 128) if narrow else (CODED, LANES)
    coded = jax.ShapeDtypeStruct((4, *shape) if step is None else shape, jnp.int16)
    packed = jax.ShapeDtypeStruct((1024, LANES), jnp.bfloat16)
    scratch = [
        pltpu.VMEM((blocks, AW, 8, 15 * 128), jnp.bfloat16),
        pltpu.VMEM((AW, 8, 128), jnp.int32),
        pltpu.VMEM((15 // GROUP, GROUP * 520, 128), jnp.float32),
        pltpu.VMEM((15 // GROUP, GROUP * AW, 1024), jnp.bfloat16),
        pltpu.VMEM((blocks, *shape), jnp.int16),
        pltpu.VMEM((8, LANES), jnp.float32),
        pltpu.SemaphoreType.DMA((4,)),
        pltpu.SemaphoreType.DMA((4,)),
    ]
    if step is None:
        scratch += [pltpu.VMEM((8, O, BJ), jnp.bfloat16), pltpu.SemaphoreType.DMA]
    elif fused:
        scratch += [pltpu.VMEM((CODED, LANES), jnp.int16), pltpu.SemaphoreType.DMA]
    return pl.pallas_call(
        functools.partial(contract_kernel, step, fused),
        grid=(1,),
        in_specs=[sm] * 5
        + [
            any_,
            pl.BlockSpec((AW, 8, 128), lambda s: (0, 0, 98)),
            pl.BlockSpec((AW, 8, 128), lambda s: (0, 0, 112)),
            vm,
            any_ if step is None else vm,
        ]
        + ([any_, any_] if fused else []),
        out_specs=[any_, vm, sm] if step is None else any_,
        scratch_shapes=scratch,
        out_shape=[coded, packed, jax.ShapeDtypeStruct((1,), jnp.int32)] if step is None else coded,
        cost_estimate=pl.CostEstimate(flops=2 * 10**9 * blocks, bytes_accessed=3 * 10**6 * blocks, transcendentals=0),
        compiler_params=pltpu.CompilerParams(vmem_limit_bytes=(44 if step is None else 24) * MIB),
        name="contract_send" if step is None else "contract_keep",
    )(first, a, b, virt, occ, amp, amp, amp, occ[None], source, *((came, after) if fused else ()))


def pair_kernel(step, own, came, out, other, sem):
    target = lax.rem(lax.axis_index("x") + step, 4)
    fetch = pltpu.make_async_copy(came.at[target], other, sem)
    fetch.start()
    fetch.wait()
    units = [read_units(block) for block in (own, other)]
    lines = []
    for g in range(3):
        power, mantissa = unit_codes(1.0001 * (units[0][g] + units[1][g]))
        inverse = 1.0 / unit_of(power, mantissa)
        lines += [power, mantissa]
        rows = slice(g * GROUP * AW, (g + 1) * GROUP * AW)
        total = own[rows, :].astype(jnp.float32) * (units[0][g] * inverse)
        total = total + other[rows, :].astype(jnp.float32) * (units[1][g] * inverse)
        put_rows(out, g, jnp.round(total))
    put_units(out, jnp.concatenate(lines + lines[:2], axis=0))


def pair(step, own, came, narrow):
    vm = pl.BlockSpec(memory_space=pltpu.VMEM)
    return pl.pallas_call(
        functools.partial(pair_kernel, step),
        in_specs=[vm, pl.BlockSpec(memory_space=pl.ANY)],
        out_specs=vm,
        out_shape=jax.ShapeDtypeStruct((NARROW, 128) if narrow else (CODED, LANES), jnp.int16),
        scratch_shapes=[pltpu.VMEM((CODED, LANES), jnp.int16), pltpu.SemaphoreType.DMA],
        compiler_params=pltpu.CompilerParams(vmem_limit_bytes=10 * MIB),
        name="pair",
    )(own, came)


def gather_kernel(one, two, three, four, out):
    blocks = (one, two, three, four)
    narrow = one.shape[0] == NARROW
    units = [read_units(block) for block in blocks]
    bounds = [units[0][g] + units[1][g] + units[2][g] + units[3][g] for g in range(3)]
    power, mantissa = unit_codes(1.0001 * jnp.maximum(jnp.maximum(bounds[0], bounds[1]), bounds[2]))
    inverse = 1.0 / unit_of(power, mantissa)
    codes = jnp.concatenate([power, mantissa, power, mantissa], axis=0)
    codes = jnp.broadcast_to(codes[None], (8, 4, LANES))

    def added(rows, columns, group):
        total = 0.0
        for block, unit in zip(blocks, units):
            total = total + block[rows, :].astype(jnp.float32) * (unit[group] * inverse)[:, columns]
        return jnp.round(total)

    high_part = [[], []]
    for quad in range(4):
        sums = []
        for inner in range(4 * quad, min(4 * quad + 4, 15)):
            rows = slice(inner * AW, (inner + 1) * AW)
            if narrow:
                total = added(rows, slice(0, 128), inner // GROUP)
                rows = slice(CODED + inner * 32, CODED + (inner + 1) * 32)
                high = added(rows, slice(128, 256), inner // GROUP)
                high = jnp.concatenate([high, pltpu.roll(high, 64, axis=1)], axis=0)
                total = jnp.concatenate([total, high], axis=1)
            else:
                total = added(rows, slice(0, 256), inner // GROUP)
            sums.append(total.reshape(8, 8, LANES))
        for half in range(2):
            rows = [s[:, 4 * half : 4 * half + 4] for s in sums] + ([codes] if quad == 3 else [])
            rows = jnp.concatenate(rows, axis=1)
            out[:, half, 16 * quad : 16 * quad + 16, :] = rows[:, :, :128].astype(jnp.int16)
            high_part[half].append(rows[:, :, 128:])
    lane = lax.broadcasted_iota(jnp.int32, (8, 16, 128), 2)
    for half in range(2):
        for quad in range(2):
            lower, upper = high_part[half][quad], high_part[half][quad + 2]
            turned = pltpu.roll(upper.reshape(128, 128), 64, axis=1).reshape(8, 16, 128)
            rows = jnp.where(lane < 64, lower, turned)
            out[:, half, 64 + 16 * quad : 80 + 16 * quad, :] = rows.astype(jnp.int16)
            if narrow:
                continue
            turned = pltpu.roll(lower.reshape(128, 128), 64, axis=1).reshape(8, 16, 128)
            rows = jnp.where(lane < 64, turned, upper)
            out[:, half, 96 + 16 * quad : 112 + 16 * quad, :] = rows.astype(jnp.int16)


def gather(*blocks):
    vm = pl.BlockSpec(memory_space=pltpu.VMEM)
    rows = 96 if blocks[0].shape[0] == NARROW else 128
    out = pl.pallas_call(
        gather_kernel,
        in_specs=[vm] * 4,
        out_specs=vm,
        out_shape=jax.ShapeDtypeStruct((8, 2, rows, 128), jnp.int16),
        compiler_params=pltpu.CompilerParams(vmem_limit_bytes=14 * MIB),
        name="gather",
    )(*blocks)
    return out.reshape(16, rows, 128)


def table_kernel(first, class_row, class_col, table):
    shape = (O, BJ)
    rank = jnp.zeros((1, BJ), jnp.float32)
    for part in range(8):
        before = lax.broadcasted_iota(jnp.int32, shape, 0) + part * O < lax.broadcasted_iota(jnp.int32, shape, 1)
        same = (class_col[part * O : (part + 1) * O, :] == class_row[...]) & before
        rank = rank + jnp.sum(jnp.where(same, 1.0, 0.0), axis=0, keepdims=True)
    slot = lax.broadcasted_iota(jnp.int32, (LANES, BJ), 0).astype(jnp.float32)
    chosen = rank - first[0].astype(jnp.float32) == slot
    table[...] = jnp.where(chosen, 1.0, 0.0).astype(jnp.bfloat16)


def make_table(first, class_row, class_col):
    vm = pl.BlockSpec(memory_space=pltpu.VMEM)
    return pl.pallas_call(
        table_kernel,
        in_specs=[pl.BlockSpec(memory_space=pltpu.SMEM), vm, vm],
        out_specs=vm,
        out_shape=jax.ShapeDtypeStruct((LANES, BJ), jnp.bfloat16),
        compiler_params=pltpu.CompilerParams(vmem_limit_bytes=14 * MIB),
        name="table",
    )(first, class_row, class_col)


BATCH = 8


def expand_kernel(narrow, came, table, class_row, row_class, out, total):
    step = pl.program_id(0)
    part = jnp.zeros(came.shape[1:], jnp.float32)
    lane = lax.broadcasted_iota(jnp.int32, (1, 128), 1)
    for n in range(BATCH):
        values = came[n].astype(jnp.float32)
        parts = [values[:64] * unit_of(values[60:61], values[61:62])]
        unit = unit_of(values[92:93], values[93:94])
        turned = pltpu.roll(unit, 64, axis=1)
        parts.append(values[64:96] * jnp.where(lane < 64, turned, unit))
        if not narrow:
            unit = unit_of(values[124:125], values[125:126])
            turned = pltpu.roll(unit, 64, axis=1)
            parts.append(values[96:] * jnp.where(lane < 64, turned, unit))
        part = part + jnp.concatenate(parts, axis=0)

    @pl.when(step == 0)
    def _():
        total[...] = part

    @pl.when(step > 0)
    def _():
        total[...] = total[...] + part

    @pl.when(step == pl.num_programs(0) - 1)
    def _():
        value = total[...]
        third = jnp.concatenate([value[64:96], pltpu.roll(value[64:96], 64, axis=1)], axis=0)
        last = 0.0
        if not narrow:
            last = jnp.concatenate([pltpu.roll(value[96:], 64, axis=1), value[96:]], axis=0)
        value = jnp.concatenate([value[:64], jnp.where(lane < 64, third, last)], axis=1)
        high = value.astype(jnp.bfloat16)
        rest = value - high.astype(jnp.float32)
        middle = rest.astype(jnp.bfloat16)
        low = (rest - middle.astype(jnp.float32)).astype(jnp.bfloat16)
        parts = jnp.concatenate([high, middle, low], axis=0)
        spread = jnp.dot(parts, table[...], preferred_element_type=jnp.float32)
        spread = spread[:64] + (spread[64:128] + spread[128:])
        out[...] = jnp.where(row_class[...] == class_row[...], spread, 0.0)[:60].reshape(15, 4, BJ)


def expand(narrow, came, table, class_row, row_class):
    whole = lambda *shape: pl.BlockSpec(shape, lambda n: (0,) * len(shape))
    sent = came.shape[1:]
    return pl.pallas_call(
        functools.partial(expand_kernel, narrow),
        grid=(came.shape[0] // BATCH,),
        in_specs=[
            pl.BlockSpec((BATCH, *sent), lambda n: (n, 0, 0)),
            whole(LANES, BJ),
            whole(1, BJ),
            whole(64, 1),
        ],
        out_specs=whole(15, 4, BJ),
        out_shape=jax.ShapeDtypeStruct((15, 4, BJ), jnp.float32),
        scratch_shapes=[pltpu.VMEM(sent, jnp.float32)],
        compiler_params=pltpu.CompilerParams(vmem_limit_bytes=14 * MIB),
        name="expand_narrow" if narrow else "expand",
    )(came, table, class_row, row_class)


def on_device(amplitudes, integrals, a_irrep, b_irrep, virt_irrep, occ_irrep):
    virt, x, core = lax.axis_index("virt"), lax.axis_index("x"), lax.axis_index("c")
    labels = a_irrep, b_irrep, virt_irrep, occ_irrep

    def finished(narrow, first, send, weights, amplitudes):
        came = lax.ppermute(send, "c", [(0, 1), (1, 0)])
        ahead = lambda step, block: lax.ppermute(block, "x", [(n, (n + step) % 4) for n in range(4)])
        keep = lambda step, *more: contract(step, first, *labels, amplitudes, weights, *more, narrow=narrow and more != ())
        two = pair(2, keep(2), came, narrow)
        one = keep(1, came, two)
        three = keep(3, came, one)
        own = keep(0, came, three)
        gathered = gather(own, ahead(2, two), ahead(1, one), ahead(3, three))
        arrived = lax.all_to_all(gathered, "virt", 0, 0, tiled=True)
        classes = (b_irrep[:, None] ^ occ_irrep[None, :]).reshape(BJ)
        class_row, class_col = classes[None, :], classes[:, None]
        a_rows = lax.dynamic_slice_in_dim(a_irrep, virt * 4, 4, 0)
        i_rows = lax.dynamic_slice_in_dim(occ_irrep, (2 * x + core) * 15, 15, 0)
        row_class = jnp.pad((i_rows[:, None] ^ a_rows[None, :]).reshape(60), (0, 4))[:, None]
        return expand(narrow, arrived, make_table(first, class_row, class_col), class_row, row_class)

    def all_passes(first, send, weights, amplitudes, fullest):
        def one_pass(number, total):
            first = (number * CAP).astype(jnp.int32)[None]
            send, weights, _ = contract(None, first, *labels, amplitudes, integrals)
            return total + finished(False, first, send, weights, amplitudes)

        passes = lax.div(fullest + (CAP - 1), CAP)
        return lax.fori_loop(1, passes, one_pass, finished(False, first, send, weights, amplitudes))

    first = jnp.zeros((1,), jnp.int32)
    send, weights, fullest = contract(None, first, *labels, amplitudes, integrals)
    total = lax.cond(
        fullest[0] <= 192,
        lambda first, send, weights, amplitudes, fullest: finished(True, first, send, weights, amplitudes),
        all_passes,
        first, send, weights, amplitudes, fullest[0],
    )
    return jnp.transpose(total, (1, 0, 2))


def solution(mesh):
    fine = Mesh(mesh.devices.reshape(16, 4, 2), ("virt", "x", "c"))
    spread = ("virt", "x", "c")
    placed = (P(None, spread, None), P(spread, None, None), P(), P(), P(), P())
    return jax.shard_map(
        on_device, mesh=fine, in_specs=placed, out_specs=P("virt", ("x", "c"), None), check_vma=False
    )
```

```python
import functools

import jax
import jax.numpy as jnp
from jax import lax
from jax.experimental import pallas as pl
from jax.experimental.pallas import tpu as pltpu
from jax.sharding import Mesh, PartitionSpec as P

O = 120
BJ = 960
AW = 64
CAP = 256
LANES = 256
MIB = 1024 * 1024


GROUP = 5
ROWS = 15 * AW
CODED = ROWS + 16


def unit_codes(unit):
    unit = jnp.maximum(unit, 1e-30)
    power = jnp.floor(jnp.log2(unit)) - 13.0
    return power, jnp.floor(unit * jnp.exp2(-power)) + 1.0


def unit_of(power, mantissa):
    return mantissa * jnp.exp2(power)


def pack_rows(first, e_labels, b_s, ints, occ_line, weights, fullest):
    diagonal = lax.broadcasted_iota(jnp.int32, (128, 128), 0) == lax.broadcasted_iota(jnp.int32, (128, 128), 1)
    occ_col = jnp.sum(jnp.where(diagonal, jnp.broadcast_to(occ_line, (128, 128)), 0), axis=1, keepdims=True)
    lane = lax.broadcasted_iota(jnp.int32, (128, BJ), 1)
    row = lax.broadcasted_iota(jnp.int32, (128, BJ), 0)
    column = lax.broadcasted_iota(jnp.int32, (1, BJ), 1)
    hit = jnp.zeros((128, BJ), jnp.bool_)
    b_row = jnp.zeros((1, BJ), jnp.int32)
    for b in range(8):
        hit = hit | (lane - b * O == row)
        b_row = jnp.where(column >= b * O, b_s[b], b_row)
    hit = hit & (row < O)
    class_row = jnp.sum(jnp.where(hit, occ_col, 0), axis=0, keepdims=True) ^ b_row
    occ_col = occ_col[:O]
    picks = []
    highest = jnp.zeros((O, 1), jnp.float32)
    for part in range(8):
        mine = lax.broadcasted_iota(jnp.int32, (O, BJ), 0) + part * O
        other = lax.broadcasted_iota(jnp.int32, (O, BJ), 1)
        same = ((occ_col ^ b_s[part]) == class_row) & (other < mine)
        rank = jnp.sum(jnp.where(same, 1.0, 0.0), axis=1, keepdims=True)
        highest = jnp.maximum(highest, rank)
        slot = lax.broadcasted_iota(jnp.int32, (O, LANES), 1).astype(jnp.float32)
        picks.append(jnp.where(rank - first.astype(jnp.float32) == slot, 1.0, 0.0))
    fullest[0] = jnp.max(highest).astype(jnp.int32) + 1
    pick = jnp.concatenate(picks, axis=0).astype(jnp.bfloat16)
    for e in range(8):
        kept = jnp.where((occ_col ^ e_labels[e]) == class_row, ints[e].astype(jnp.float32), 0.0)
        packed = jnp.dot(kept.astype(jnp.bfloat16), pick, preferred_element_type=jnp.float32)
        whole = jnp.concatenate([packed, jnp.zeros((128 - O, LANES), jnp.float32)], axis=0)
        weights[e * 128 : (e + 1) * 128, :] = whole.astype(jnp.bfloat16)


NARROW = CODED + ROWS // 2 + 16


def doubled(rows):
    lane = lax.broadcasted_iota(jnp.int32, rows.shape, 1)
    return jnp.where(lane < 64, rows, pltpu.roll(rows, 64, axis=1))


def read_units(block):
    narrow = block.shape[0] == NARROW
    lines = block[ROWS:CODED, :].astype(jnp.float32)
    if narrow:
        lines = jnp.concatenate([lines, block[NARROW - 16 :, :].astype(jnp.float32)], axis=1)
    return [unit_of(lines[2 * g : 2 * g + 1], lines[2 * g + 1 : 2 * g + 2]) for g in range(3)]


def put_rows(out, group, coded):
    size = GROUP * AW
    if out.shape[0] == CODED:
        out[group * size : (group + 1) * size, :] = coded.astype(jnp.int16)
        return
    out[group * size : (group + 1) * size, :] = coded[:, :128].astype(jnp.int16)
    high = coded[:, 128:].reshape(GROUP, AW, 128)
    lower, upper = (part.reshape(size // 2, 128) for part in (high[:, :32], high[:, 32:]))
    lane = lax.broadcasted_iota(jnp.int32, lower.shape, 1)
    rows = jnp.where(lane < 64, lower, pltpu.roll(upper, 64, axis=1))
    start = CODED + group * size // 2
    out[start : start + size // 2, :] = rows.astype(jnp.int16)


def put_units(out, lines):
    lines = jnp.concatenate([lines, lines], axis=0)
    if out.shape[0] == CODED:
        out[ROWS:, :] = lines.astype(jnp.int16)
        return
    out[ROWS:CODED, :] = lines[:, :128].astype(jnp.int16)
    out[NARROW - 16 :, :] = doubled(lines[:, 128:]).astype(jnp.int16)


def contract_kernel(step, fused, first, a_s, b_s, virt_s, occ_s, amp, *rest):
    came = edge = None
    if step is None:
        edge, *rest = rest
    last, occ_in, source, *rest = rest
    if step is None:
        out, weights, fullest, buf, labels, stage, left, codes, lines, in_sems, out_sems, ints, ints_sem = rest
    elif fused:
        came, _, out, buf, labels, stage, left, codes, lines, in_sems, out_sems, other, other_sem = rest
        weights = source
    else:
        out, buf, labels, stage, left, codes, lines, in_sems, out_sems = rest
        weights = source
    core = lax.axis_index("c")
    my_x = lax.axis_index("x")
    device = (lax.axis_index("virt") * 4 + my_x) * 2 + core
    half = 1 - core if step is None else core
    target = None if step is None else lax.rem(my_x + step, 4)

    def read(x):
        start = pl.multiple_of(128 * (28 * x + 14 * half), 128)
        size = 1792 if x == 3 else 1920
        return pltpu.make_async_copy(
            amp.at[:, :, pl.ds(start, size)], buf.at[x, :, :, pl.ds(0, size)], in_sems.at[x]
        )

    if step is None:
        reads = [read(x) for x in range(4)]
    else:
        tile = 28 * target + 14 * half
        reads = [
            pltpu.make_async_copy(
                amp.at[:, :, pl.ds(pl.multiple_of(128 * (tile + begin), 128), 128 * size)],
                buf.at[0, :, :, pl.ds(128 * begin, 128 * size)],
                in_sems.at[n],
            )
            for n, (begin, size) in enumerate(((0, 7), (7, 4), (11, 3)))
        ] + [
            pltpu.make_async_copy(
                amp.at[:, :, pl.ds(pl.multiple_of(128 * jnp.minimum(tile + 14, 111), 128), 128)],
                buf.at[0, :, :, pl.ds(1792, 128)],
                in_sems.at[3],
            ),
        ]
    e_labels = [virt_s[device * 8 + e] for e in range(8)]
    if step is None:
        fetch = pltpu.make_async_copy(source, ints, ints_sem)
        fetch.start()
    for n in range(2 if step is None else 4):
        reads[n].start()
    if fused:
        fetch = pltpu.make_async_copy(came.at[target], other, other_sem)
        fetch.start()
    lines[...] = jnp.zeros_like(lines)
    lines[0:1, :O] = occ_in[...].astype(jnp.float32)
    occ_line = lines[0:1, :128].astype(jnp.int32)
    row = lax.broadcasted_iota(jnp.int32, (8, 128), 0)
    e_label = jnp.zeros((8, 128), jnp.int32)
    for e in range(8):
        e_label = jnp.where(row == e, e_labels[e], e_label)
    for a in range(AW):
        labels[a] = e_label ^ a_s[a]
    if step is None:
        buf[3, :, :, 1792:] = jnp.where(half == 0, edge[...], last[...])
        fetch.wait()
        pack_rows(first[0], e_labels, b_s, ints, occ_line, weights, fullest)
    lane = lax.broadcasted_iota(jnp.int32, (AW, 8, 128), 2)
    lanes = lax.broadcasted_iota(jnp.int32, (8, 128), 1)
    occ_rows = jnp.where(lanes < O, jnp.broadcast_to(occ_line, (8, 128)), 64)

    def groups(x, slot, units, ready):
        for number in range(15 // GROUP):
            ready(number)
            for u in range(GROUP):
                inner = number * GROUP + u
                flat = 16 * x + 8 * half + O * inner
                tile = lax.div(flat, 128)
                offset = flat - 128 * tile
                now = buf[slot, :, :, pl.ds(pl.multiple_of(tile * 128, 128), 128)].astype(jnp.float32)
                after = buf[slot, :, :, pl.ds(pl.multiple_of(tile * 128 + 128, 128), 128)].astype(jnp.float32)
                row = pltpu.roll(jnp.where(lane >= offset, now, after), lax.rem(128 - offset, 128), axis=2)
                pair = occ_rows ^ occ_s[30 * x + 15 * half + inner]
                row = jnp.where(labels[...] == pair[None], row, 0.0)
                for a in range(AW):
                    stage[number, pl.ds(u * 520 + a, 8, stride=65), :] = row[a]
                for e in range(8):
                    rows = stage[number, pl.ds(u * 520 + 65 * e, AW), :]
                    left[number, u * AW : (u + 1) * AW, e * 128 : (e + 1) * 128] = rows.astype(jnp.bfloat16)
            mine = slice(number * GROUP * AW, (number + 1) * GROUP * AW)
            total = jnp.dot(left[number], weights[...], preferred_element_type=jnp.float32)
            if fused:
                total = total + other[mine, :].astype(jnp.float32) * units[number]
            largest = jnp.max(jnp.abs(total), axis=0, keepdims=True)
            power, mantissa = unit_codes(largest * (1.0001 / 32767.0))
            lines[2 * number : 2 * number + 1, :] = power
            lines[2 * number + 1 : 2 * number + 2, :] = mantissa
            coded = jnp.round(total * (1.0 / unit_of(power, mantissa)))
            put_rows(codes.at[slot], number, coded)
        put_units(codes.at[slot], lines[...])

    if step is not None:
        def ready(number):
            if number == 0:
                reads[0].wait()
            if number == 1:
                for n in range(1, 4):
                    reads[n].wait()

                @pl.when((target == 3) & (half == 1))
                def _():
                    buf[0, :, :, 1792:] = last[...]

        units = None
        if fused:
            fetch.wait()
            units = read_units(other)
        groups(target, 0, units, ready)
        write = pltpu.make_async_copy(codes.at[0], out, out_sems.at[0])
        write.start()
        write.wait()
        return

    def write(x):
        return pltpu.make_async_copy(codes.at[x], out.at[x], out_sems.at[x])

    def block(x, carry):
        for n in range(4):

            @pl.when(x == n)
            def _():
                reads[n].wait()
                if n < 2:
                    reads[n + 2].start()

        groups(x, x, None, lambda number: None)
        write(x).start()
        return carry

    lax.fori_loop(0, 4, block, 0)
    for x in range(4):
        write(x).wait()


def contract(step, first, a, b, virt, occ, amp, source, came=None, after=None, narrow=False):
    any_, sm, vm = (pl.BlockSpec(memory_space=space) for space in (pl.ANY, pltpu.SMEM, pltpu.VMEM))
    fused = came is not None
    blocks = 4 if step is None else 1
    shape = (NARROW, 128) if narrow else (CODED, LANES)
    coded = jax.ShapeDtypeStruct((4, *shape) if step is None else shape, jnp.int16)
    packed = jax.ShapeDtypeStruct((1024, LANES), jnp.bfloat16)
    scratch = [
        pltpu.VMEM((blocks, AW, 8, 15 * 128), jnp.bfloat16),
        pltpu.VMEM((AW, 8, 128), jnp.int32),
        pltpu.VMEM((15 // GROUP, GROUP * 520, 128), jnp.float32),
        pltpu.VMEM((15 // GROUP, GROUP * AW, 1024), jnp.bfloat16),
        pltpu.VMEM((blocks, *shape), jnp.int16),
        pltpu.VMEM((8, LANES), jnp.float32),
        pltpu.SemaphoreType.DMA((4,)),
        pltpu.SemaphoreType.DMA((4,)),
    ]
    if step is None:
        scratch += [pltpu.VMEM((8, O, BJ), jnp.bfloat16), pltpu.SemaphoreType.DMA]
    elif fused:
        scratch += [pltpu.VMEM((CODED, LANES), jnp.int16), pltpu.SemaphoreType.DMA]
    return pl.pallas_call(
        functools.partial(contract_kernel, step, fused),
        grid=(1,),
        in_specs=[sm] * 5
        + [
            any_,
            *([pl.BlockSpec((AW, 8, 128), lambda s: (0, 0, 98))] if step is None else []),
            pl.BlockSpec((AW, 8, 128), lambda s: (0, 0, 112)),
            vm,
            any_ if step is None else vm,
        ]
        + ([any_, any_] if fused else []),
        out_specs=[any_, vm, sm] if step is None else any_,
        scratch_shapes=scratch,
        out_shape=[coded, packed, jax.ShapeDtypeStruct((1,), jnp.int32)] if step is None else coded,
        cost_estimate=pl.CostEstimate(flops=2 * 10**9 * blocks, bytes_accessed=3 * 10**6 * blocks, transcendentals=0),
        compiler_params=pltpu.CompilerParams(vmem_limit_bytes=(44 if step is None else 24) * MIB),
        name="contract_send" if step is None else "contract_keep",
    )(first, a, b, virt, occ, amp, amp, *((amp,) if step is None else ()), occ[None], source, *((came, after) if fused else ()))


def pair_kernel(step, own, came, out, other, sem):
    target = lax.rem(lax.axis_index("x") + step, 4)
    fetch = pltpu.make_async_copy(came.at[target], other, sem)
    fetch.start()
    fetch.wait()
    units = [read_units(block) for block in (own, other)]
    lines = []
    for g in range(3):
        power, mantissa = unit_codes(1.0001 * (units[0][g] + units[1][g]))
        inverse = 1.0 / unit_of(power, mantissa)
        lines += [power, mantissa]
        rows = slice(g * GROUP * AW, (g + 1) * GROUP * AW)
        total = own[rows, :].astype(jnp.float32) * (units[0][g] * inverse)
        total = total + other[rows, :].astype(jnp.float32) * (units[1][g] * inverse)
        put_rows(out, g, jnp.round(total))
    put_units(out, jnp.concatenate(lines + lines[:2], axis=0))


def pair(step, own, came, narrow):
    vm = pl.BlockSpec(memory_space=pltpu.VMEM)
    return pl.pallas_call(
        functools.partial(pair_kernel, step),
        in_specs=[vm, pl.BlockSpec(memory_space=pl.ANY)],
        out_specs=vm,
        out_shape=jax.ShapeDtypeStruct((NARROW, 128) if narrow else (CODED, LANES), jnp.int16),
        scratch_shapes=[pltpu.VMEM((CODED, LANES), jnp.int16), pltpu.SemaphoreType.DMA],
        compiler_params=pltpu.CompilerParams(vmem_limit_bytes=10 * MIB),
        name="pair",
    )(own, came)


def gather_kernel(one, two, three, four, out):
    blocks = (one, two, three, four)
    narrow = one.shape[0] == NARROW
    units = [read_units(block) for block in blocks]
    bounds = [units[0][g] + units[1][g] + units[2][g] + units[3][g] for g in range(3)]
    power, mantissa = unit_codes(1.0001 * jnp.maximum(jnp.maximum(bounds[0], bounds[1]), bounds[2]))
    inverse = 1.0 / unit_of(power, mantissa)
    codes = jnp.concatenate([power, mantissa, power, mantissa], axis=0)
    codes = jnp.broadcast_to(codes[None], (8, 4, LANES))

    def added(rows, columns, group):
        total = 0.0
        for block, unit in zip(blocks, units):
            total = total + block[rows, :].astype(jnp.float32) * (unit[group] * inverse)[:, columns]
        return jnp.round(total)

    high_part = [[], []]
    for quad in range(4):
        sums = []
        for inner in range(4 * quad, min(4 * quad + 4, 15)):
            rows = slice(inner * AW, (inner + 1) * AW)
            if narrow:
                total = added(rows, slice(0, 128), inner // GROUP)
                rows = slice(CODED + inner * 32, CODED + (inner + 1) * 32)
                high = added(rows, slice(128, 256), inner // GROUP)
                high = jnp.concatenate([high, pltpu.roll(high, 64, axis=1)], axis=0)
                total = jnp.concatenate([total, high], axis=1)
            else:
                total = added(rows, slice(0, 256), inner // GROUP)
            sums.append(total.reshape(8, 8, LANES))
        for half in range(2):
            rows = [s[:, 4 * half : 4 * half + 4] for s in sums] + ([codes] if quad == 3 else [])
            rows = jnp.concatenate(rows, axis=1)
            out[:, half, 16 * quad : 16 * quad + 16, :] = rows[:, :, :128].astype(jnp.int16)
            high_part[half].append(rows[:, :, 128:])
    lane = lax.broadcasted_iota(jnp.int32, (8, 16, 128), 2)
    for half in range(2):
        for quad in range(2):
            lower, upper = high_part[half][quad], high_part[half][quad + 2]
            turned = pltpu.roll(upper.reshape(128, 128), 64, axis=1).reshape(8, 16, 128)
            rows = jnp.where(lane < 64, lower, turned)
            out[:, half, 64 + 16 * quad : 80 + 16 * quad, :] = rows.astype(jnp.int16)
            if narrow:
                continue
            turned = pltpu.roll(lower.reshape(128, 128), 64, axis=1).reshape(8, 16, 128)
            rows = jnp.where(lane < 64, turned, upper)
            out[:, half, 96 + 16 * quad : 112 + 16 * quad, :] = rows.astype(jnp.int16)


def gather(*blocks):
    vm = pl.BlockSpec(memory_space=pltpu.VMEM)
    rows = 96 if blocks[0].shape[0] == NARROW else 128
    out = pl.pallas_call(
        gather_kernel,
        in_specs=[vm] * 4,
        out_specs=vm,
        out_shape=jax.ShapeDtypeStruct((8, 2, rows, 128), jnp.int16),
        compiler_params=pltpu.CompilerParams(vmem_limit_bytes=14 * MIB),
        name="gather",
    )(*blocks)
    return out.reshape(16, rows, 128)


def table_kernel(first, class_row, class_col, table):
    shape = (O, BJ)
    rank = jnp.zeros((1, BJ), jnp.float32)
    for part in range(8):
        before = lax.broadcasted_iota(jnp.int32, shape, 0) + part * O < lax.broadcasted_iota(jnp.int32, shape, 1)
        same = (class_col[part * O : (part + 1) * O, :] == class_row[...]) & before
        rank = rank + jnp.sum(jnp.where(same, 1.0, 0.0), axis=0, keepdims=True)
    slot = lax.broadcasted_iota(jnp.int32, (LANES, BJ), 0).astype(jnp.float32)
    chosen = rank - first[0].astype(jnp.float32) == slot
    table[...] = jnp.where(chosen, 1.0, 0.0).astype(jnp.bfloat16)


def make_table(first, class_row, class_col):
    vm = pl.BlockSpec(memory_space=pltpu.VMEM)
    return pl.pallas_call(
        table_kernel,
        in_specs=[pl.BlockSpec(memory_space=pltpu.SMEM), vm, vm],
        out_specs=vm,
        out_shape=jax.ShapeDtypeStruct((LANES, BJ), jnp.bfloat16),
        compiler_params=pltpu.CompilerParams(vmem_limit_bytes=14 * MIB),
        name="table",
    )(first, class_row, class_col)


BATCH = 16


def expand_kernel(narrow, came, table, class_row, row_class, out, total):
    step = pl.program_id(0)
    part = jnp.zeros(came.shape[1:], jnp.float32)
    lane = lax.broadcasted_iota(jnp.int32, (1, 128), 1)
    for n in range(BATCH):
        values = came[n].astype(jnp.float32)
        parts = [values[:64] * unit_of(values[60:61], values[61:62])]
        unit = unit_of(values[92:93], values[93:94])
        turned = pltpu.roll(unit, 64, axis=1)
        parts.append(values[64:96] * jnp.where(lane < 64, turned, unit))
        if not narrow:
            unit = unit_of(values[124:125], values[125:126])
            turned = pltpu.roll(unit, 64, axis=1)
            parts.append(values[96:] * jnp.where(lane < 64, turned, unit))
        part = part + jnp.concatenate(parts, axis=0)

    @pl.when(step == 0)
    def _():
        total[...] = part

    @pl.when(step > 0)
    def _():
        total[...] = total[...] + part

    @pl.when(step == pl.num_programs(0) - 1)
    def _():
        value = total[...]
        third = jnp.concatenate([value[64:96], pltpu.roll(value[64:96], 64, axis=1)], axis=0)
        last = 0.0
        if not narrow:
            last = jnp.concatenate([pltpu.roll(value[96:], 64, axis=1), value[96:]], axis=0)
        value = jnp.concatenate([value[:64], jnp.where(lane < 64, third, last)], axis=1)
        high = value.astype(jnp.bfloat16)
        rest = value - high.astype(jnp.float32)
        middle = rest.astype(jnp.bfloat16)
        low = (rest - middle.astype(jnp.float32)).astype(jnp.bfloat16)
        parts = jnp.concatenate([high, middle, low], axis=0)
        spread = jnp.dot(parts, table[...], preferred_element_type=jnp.float32)
        spread = spread[:64] + (spread[64:128] + spread[128:])
        out[...] = jnp.where(row_class[...] == class_row[...], spread, 0.0)[:60].reshape(15, 4, BJ)


def expand(narrow, came, table, class_row, row_class):
    whole = lambda *shape: pl.BlockSpec(shape, lambda n: (0,) * len(shape))
    sent = came.shape[1:]
    return pl.pallas_call(
        functools.partial(expand_kernel, narrow),
        grid=(came.shape[0] // BATCH,),
        in_specs=[
            pl.BlockSpec((BATCH, *sent), lambda n: (n, 0, 0)),
            whole(LANES, BJ),
            whole(1, BJ),
            whole(64, 1),
        ],
        out_specs=whole(15, 4, BJ),
        out_shape=jax.ShapeDtypeStruct((15, 4, BJ), jnp.float32),
        scratch_shapes=[pltpu.VMEM(sent, jnp.float32)],
        compiler_params=pltpu.CompilerParams(vmem_limit_bytes=14 * MIB),
        name="expand_narrow" if narrow else "expand",
    )(came, table, class_row, row_class)


def on_device(amplitudes, integrals, a_irrep, b_irrep, virt_irrep, occ_irrep):
    virt, x, core = lax.axis_index("virt"), lax.axis_index("x"), lax.axis_index("c")
    labels = a_irrep, b_irrep, virt_irrep, occ_irrep

    def finished(narrow, first, send, weights, amplitudes):
        came = lax.ppermute(send, "c", [(0, 1), (1, 0)])
        ahead = lambda step, block: lax.ppermute(block, "x", [(n, (n + step) % 4) for n in range(4)])
        keep = lambda step, *more: contract(step, first, *labels, amplitudes, weights, *more, narrow=narrow and more != ())
        two = pair(2, keep(2), came, narrow)
        one = keep(1, came, two)
        three = keep(3, came, one)
        own = keep(0, came, three)
        gathered = gather(own, ahead(2, two), ahead(1, one), ahead(3, three))
        arrived = lax.all_to_all(gathered, "virt", 0, 0, tiled=True)
        classes = (b_irrep[:, None] ^ occ_irrep[None, :]).reshape(BJ)
        class_row, class_col = classes[None, :], classes[:, None]
        a_rows = lax.dynamic_slice_in_dim(a_irrep, virt * 4, 4, 0)
        i_rows = lax.dynamic_slice_in_dim(occ_irrep, (2 * x + core) * 15, 15, 0)
        row_class = jnp.pad((i_rows[:, None] ^ a_rows[None, :]).reshape(60), (0, 4))[:, None]
        return expand(narrow, arrived, make_table(first, class_row, class_col), class_row, row_class)

    def all_passes(first, send, weights, amplitudes, fullest):
        def one_pass(number, total):
            first = (number * CAP).astype(jnp.int32)[None]
            send, weights, _ = contract(None, first, *labels, amplitudes, integrals)
            return total + finished(False, first, send, weights, amplitudes)

        passes = lax.div(fullest + (CAP - 1), CAP)
        return lax.fori_loop(1, passes, one_pass, finished(False, first, send, weights, amplitudes))

    first = jnp.zeros((1,), jnp.int32)
    send, weights, fullest = contract(None, first, *labels, amplitudes, integrals)
    total = lax.cond(
        fullest[0] <= 192,
        lambda first, send, weights, amplitudes, fullest: finished(True, first, send, weights, amplitudes),
        all_passes,
        first, send, weights, amplitudes, fullest[0],
    )
    return jnp.transpose(total, (1, 0, 2))


def solution(mesh):
    fine = Mesh(mesh.devices.reshape(16, 4, 2), ("virt", "x", "c"))
    spread = ("virt", "x", "c")
    placed = (P(None, spread, None), P(spread, None, None), P(), P(), P(), P())
    return jax.shard_map(
        on_device, mesh=fine, in_specs=placed, out_specs=P("virt", ("x", "c"), None), check_vma=False
    )
```
